256 devices in a mesh: lev: 4 (over y_lo, core), tile: 64 (over x, y_hi, z).
Axes of the slice: x: 4, y: 4 (y_hi: 2, y_lo: 2; y = y_hi * 2 + y_lo), z: 8, core: 2. Of those that a mesh axis runs over, the one named last changes fastest.
Arguments:
- control: float32 [96, 64, 256], P(None, 'tile'), may hold values from -6 to 6
- emit_mask: int32 [64, 256], P('tile'), may hold values 0 or 1
- bin_profile: float32 [96], replicated, may hold values from 0.2 to 2
- plume_profile: float32 [64], P('lev'), may hold values from 0.2 to 2
- courant: float32 [2, 64, 64, 256], P(None, 'lev', 'tile'), may hold values from 0.05 to 0.24
- upwind: int32 [2, 64, 64, 256], P(None, 'lev', 'tile'), may hold values from 0 to 1
- bin_speed: float32 [96], replicated, may hold values from 0.2 to 1000
- level_factor: float32 [64], replicated, may hold values from 0.4 to 1.6
- background: float32 [96, 64, 64, 256], P(None, 'lev', 'tile'), may hold values from 0.1 to 1
- coag_rate: float32 [64, 64, 256], P('lev', 'tile'), may hold values from 0.002 to 0.01
- obs_weight: float32 [96], replicated, may hold values from 0.2 to 2
- obs_precision: float32 [64, 256], P('tile'), may hold values from 0.5 to 2
Outputs:
- obs_tangent: float32 [64, 256], P('tile')
- hess_vec: float32 [96, 64, 256], P(None, 'tile')
The draws below stay inside these ranges and needn't reach their ends.
Inputs may be any that keep to these rules, and one draw needn't show every extreme that they name: `emit_mask`: 1 marks an emitting column.
All inputs are finite; a program needn't handle non-finite values. No bound on the sum of `emit_mask` on one device may be relied on, other than what follows from the above.
Results may differ from the reference program's by a relative error of at most 0.0003.
Values sent between devices are 32-bit elements; how exact they have to be, the bound alone decides.
A program may use at most 64 MiB of HBM per device.

```python
import math
import jax
import jax.numpy as jnp
from jax import lax

NB = 96
NY = 256
NX = 64
LEVELS = 64


def with_ends(array, stream_key, smallest, high):
    shape = array.shape
    index_at = [jax.random.randint(jax.random.fold_in(stream_key, axis), (), 0, shape[axis]) for axis in range(len(shape))]
    array = array.at[tuple(index_at)].set(smallest)
    longest = shape.index(max(shape))
    index_at[longest] = (index_at[longest] + 1) % shape[longest]
    return array.at[tuple(index_at)].set(high)


def block_scale(own_key, shape, cuts, smallest, top_value):
    level, own = 1.0, jax.random.fold_in(own_key, 6)
    for axis_at, shards_of in cuts:
        heights = jnp.exp(jax.random.uniform(jax.random.fold_in(own, axis_at), (shards_of,), jnp.float32, smallest / len(cuts), top_value / len(cuts)))
        level = level * jnp.repeat(heights, shape[axis_at] // shards_of).reshape([-1 if axis == axis_at else 1 for axis in range(len(shape))])
    return level


def scatter_about(own_key, dims, width, reach, cuts=(), held_as=jnp.bfloat16):
    entries = width * jax.random.normal(own_key, dims, jnp.float32)
    if cuts:
        entries = entries * block_scale(own_key, dims, cuts, -0.22, 0.18)
    return jnp.clip(entries, -reach, reach).astype(held_as)


def setup_inputs(seed: int = 0) -> dict:
    keys = jax.random.split(jax.random.key(seed), 13)
    control = scatter_about(keys[0], (NB, NX, NY), 1.0, 6.0, ((1, 64),), jnp.float32)
    emit_mask = with_ends((jax.random.randint(keys[1], (NX, NY), 0, 2) < 1).astype(jnp.int32), jax.random.fold_in(keys[1], 1), 0, 1)
    bin_profile = jnp.clip(jnp.exp(jax.random.uniform(keys[2], (NB,), jnp.float32, math.log(0.2), math.log(2.0))), 0.2, 2.0)
    plume_profile = jnp.clip(jnp.exp(math.log(2.0) - 2.3025851 * jax.random.uniform(keys[3], (LEVELS,), jnp.float32) ** block_scale(keys[3], (LEVELS,), ((0, 4),), -0.2, 0.2)), 0.2, 2.0)
    courant = jnp.clip(0.05 + 0.19 * jax.random.uniform(keys[4], (2, LEVELS, NX, NY), jnp.float32) ** block_scale(keys[4], (2, LEVELS, NX, NY), ((1, 4), (2, 64)), -0.2, 0.2), 0.05, 0.24)
    upwind = with_ends(jax.random.randint(keys[5], (2, LEVELS, NX, NY), 0, 2), jax.random.fold_in(keys[5], 1), 0, 1).astype(jnp.int32)
    bin_speed = jnp.clip(jnp.exp(jax.random.uniform(keys[6], (NB,), jnp.float32, math.log(0.2), math.log(1000.0))), 0.2, 1000.0)
    level_factor = jnp.clip(1.0 + 0.12 * jax.random.normal(keys[7], (LEVELS,), jnp.float32), 0.4, 1.6)
    background = jnp.clip(0.1 + 0.9 * jax.random.uniform(keys[8], (NB, LEVELS, NX, NY), jnp.float32) ** block_scale(keys[8], (NB, LEVELS, NX, NY), ((1, 4), (2, 64)), -0.2, 0.2), 0.1, 1.0)
    coag_rate = jnp.clip(jnp.exp(math.log(0.01) - 1.6094378 * jax.random.uniform(keys[9], (LEVELS, NX, NY), jnp.float32) ** block_scale(keys[9], (LEVELS, NX, NY), ((0, 4), (1, 64)), -0.2, 0.2)), 0.002, 0.01)
    obs_weight = jnp.clip(jnp.exp(jax.random.uniform(keys[10], (NB,), jnp.float32, math.log(0.2), math.log(2.0))), 0.2, 2.0)
    obs_precision = jnp.clip(jnp.exp(math.log(2.0) - 1.3862944 * jax.random.uniform(keys[11], (NX, NY), jnp.float32) ** block_scale(keys[11], (NX, NY), ((0, 64),), -0.2, 0.2)), 0.5, 2.0)
    return dict(control=control, emit_mask=emit_mask, bin_profile=bin_profile, plume_profile=plume_profile, courant=courant, upwind=upwind, bin_speed=bin_speed, level_factor=level_factor, background=background, coag_rate=coag_rate, obs_weight=obs_weight, obs_precision=obs_precision)


def spectrum(values_in):
    return jnp.fft.rfft(values_in, n=2 * NB, axis=0)


def advect(tangent, signed):
    face_x = signed[0][None]
    face_y = signed[1][None]
    flux_x = face_x * jnp.where(face_x > 0, jnp.roll(tangent, 1, axis=2), tangent)
    flux_y = face_y * jnp.where(face_y > 0, jnp.roll(tangent, 1, axis=3), tangent)
    return tangent + flux_x - jnp.roll(flux_x, -1, axis=2) + flux_y - jnp.roll(flux_y, -1, axis=3)


def advect_adjoint(adjoint, signed):
    face_x = signed[0][None]
    face_y = signed[1][None]
    term_x = face_x * (adjoint - jnp.roll(adjoint, 1, axis=2))
    term_y = face_y * (adjoint - jnp.roll(adjoint, 1, axis=3))
    result = adjoint + jnp.where(face_x < 0, term_x, 0.0) + jnp.roll(jnp.where(face_x > 0, term_x, 0.0), -1, axis=2)
    return result + jnp.where(face_y < 0, term_y, 0.0) + jnp.roll(jnp.where(face_y > 0, term_y, 0.0), -1, axis=3)


def settle(tangent, fall_speed):
    zeros_col = jnp.zeros((fall_speed.shape[0], 1), fall_speed.dtype)
    above = jnp.concatenate([fall_speed[:, 1:], zeros_col], axis=1)
    above_lev = jnp.moveaxis(above, 1, 0)[:, :, None, None]
    speed_lev = jnp.moveaxis(fall_speed, 1, 0)[:, :, None, None]

    def sweep_level(carry_in, pieces):
        layer_in, above_here, speed_here = pieces
        carry_out = (layer_in + above_here * carry_in) / (1.0 + speed_here)
        return carry_out, carry_out

    finished, stacked = lax.scan(sweep_level, jnp.zeros_like(tangent[:, 0]), (jnp.moveaxis(tangent, 1, 0), above_lev, speed_lev), reverse=True)
    return jnp.moveaxis(stacked, 0, 1)


def settle_adjoint(adjoint, fall_speed):
    speed_lev = jnp.moveaxis(fall_speed, 1, 0)[:, :, None, None]

    def sweep_level(carry_in, pieces):
        layer_in, speed_here = pieces
        carry_out = (layer_in + speed_here * carry_in) / (1.0 + speed_here)
        return carry_out, carry_out

    finished, stacked = lax.scan(sweep_level, jnp.zeros_like(adjoint[:, 0]), (jnp.moveaxis(adjoint, 1, 0), speed_lev))
    return jnp.moveaxis(stacked, 0, 1)


def coagulate(values_all, background, coag_rate, adjoint_mode):
    def per_level(pieces):
        values_in, back_level, rate_level = pieces
        back_spec = spectrum(back_level)
        if adjoint_mode:
            back_spec = jnp.conj(back_spec)
        gain_term = jnp.fft.irfft(back_spec * spectrum(values_in), n=2 * NB, axis=0)[:NB]
        back_total = jnp.sum(back_level, axis=0)[None]
        if adjoint_mode:
            loss_term = jnp.sum(back_level * values_in, axis=0)[None] + values_in * back_total
        else:
            loss_term = back_level * jnp.sum(values_in, axis=0)[None] + values_in * back_total
        return values_in + rate_level[None] * (gain_term - loss_term)

    mapped = lax.map(per_level, (jnp.swapaxes(values_all, 0, 1), jnp.swapaxes(background, 0, 1), coag_rate))
    return jnp.swapaxes(mapped, 0, 1)


def reference(control, emit_mask, bin_profile, plume_profile, courant, upwind, bin_speed, level_factor, background, coag_rate, obs_weight, obs_precision):
    signed = jnp.where(upwind == 1, courant, -courant)
    fall_speed = bin_speed[:, None] * level_factor[None, :]
    mask_float = emit_mask.astype(jnp.float32)
    masked = control * mask_float[None]
    weights = bin_profile[:, None] * plume_profile[None, :]
    source = weights[:, :, None, None] * masked[:, None]
    tangent = advect(source, signed)
    tangent = settle(tangent, fall_speed)
    tangent = coagulate(tangent, background, coag_rate, False)
    inv_count = 1.0 / (NB * LEVELS)
    obs_tangent = jnp.sum(obs_weight[:, None, None, None] * tangent, axis=(0, 1)) * inv_count
    adjoint = obs_weight[:, None, None, None] * (obs_precision * obs_tangent * inv_count)[None, None]
    adjoint = jnp.broadcast_to(adjoint, tangent.shape)
    adjoint = coagulate(adjoint, background, coag_rate, True)
    adjoint = settle_adjoint(adjoint, fall_speed)
    adjoint = advect_adjoint(adjoint, signed)
    hess_vec = mask_float[None] * jnp.sum(weights[:, :, None, None] * adjoint, axis=1)
    return obs_tangent, hess_vec
```

```python
import functools

import jax
import jax.numpy as jnp
from jax import lax
from jax.experimental import pallas as pl
from jax.experimental.pallas import tpu as pltpu
from jax.sharding import PartitionSpec as P

MESH = pl.DeviceIdType.MESH
F32, BF16 = jnp.float32, jnp.bfloat16


def split(value):
    high = value.astype(BF16)
    return high, (value - high.astype(F32)).astype(BF16)


def dot3(a, b):
    a_hi, a_lo = split(a)
    b_hi, b_lo = split(b)
    dot = functools.partial(jnp.dot, preferred_element_type=F32)
    return dot(a_hi, b_hi) + (dot(a_hi, b_lo) + dot(a_lo, b_hi))


def iota(shape, dim):
    return lax.broadcasted_iota(jnp.int32, shape, dim)


def pad_row(row, lanes):
    return jnp.concatenate([row, jnp.zeros((1, lanes - row.shape[1]), row.dtype)], axis=1)


def column(row, rows):
    shape = (rows, row.shape[1])
    picked = jnp.where(iota(shape, 0) == iota(shape, 1), jnp.broadcast_to(row, shape), 0.0)
    return jnp.sum(picked, axis=1, keepdims=True)


def kernel(
    nb, nl, total, scale,
    control, mask_in, profile_in, plume_in, courant, upwind, speed_in, factor_in, background, rate_in, weight_in, prec_in,
    obs_out, hess_out,
    bg, ctl, mask, profile, plume, cour, upw, speed, factor, rate, weight, prec,
    lhs, amp, rb, gb, bfield, face, nface, coef, ncoef, quot, nquot, masked, edge, kern,
    du_in, self_in, left_in, right_in, t_lev, t_left, t_right, t_own, s_own, out_buf,
    load_sem, bg_sem,
    halo_send, halo_recv, down_send, down_recv, edge_send, edge_recv,
    du_send, du_recv, self_send, self_recv, left_send, left_recv, right_send, right_recv,
    tl_send, tl_recv, tx_send, tx_recv, ag_send, ag_recv,
):
    lev, tile = lax.axis_index("lev"), lax.axis_index("tile")
    tiles = lax.axis_size("tile")
    before, after = lax.rem(tile + tiles - 1, tiles), lax.rem(tile + 1, tiles)
    ny = bg.shape[2]
    chunk = nb // 4

    def at(lev_to, tile_to):
        return {"lev": lev_to, "tile": tile_to}

    def send(src, dst, send_sem, recv_sem, lev_to, tile_to):
        return pltpu.make_async_remote_copy(
            src_ref=src, dst_ref=dst, send_sem=send_sem, recv_sem=recv_sem,
            device_id=at(lev_to, tile_to), device_id_type=MESH,
        )

    def arrived(dst, sem):
        pltpu.make_async_copy(dst, dst, sem).wait()

    small = [
        (courant.at[:, :, 0, :], cour), (upwind.at[:, :, 0, :], upw), (plume_in, plume), (control.at[:, 0, :], ctl),
        (mask_in, mask), (speed_in, speed), (factor_in, factor), (weight_in, weight), (profile_in, profile),
        (rate_in.at[:, 0, :], rate), (prec_in, prec),
    ]
    loads = [pltpu.make_async_copy(a, b, load_sem.at[n]) for n, (a, b) in enumerate(small)]
    for copy in loads:
        copy.start()

    def bg_copy(l):
        return pltpu.make_async_copy(background.at[:, l, 0, :], bg.at[l], bg_sem.at[l])

    def bg_start(l, _):
        bg_copy(l).start()
        return 0

    lax.fori_loop(0, nl, bg_start, 0)

    barrier = pltpu.get_barrier_semaphore()
    for k in range(1, 4):
        pl.semaphore_signal(barrier, inc=1, device_id=at(lev ^ k, tile), device_id_type=MESH)
    for near in (before, after):
        for k in range(4):
            pl.semaphore_signal(barrier, inc=1, device_id=at(k, near), device_id_type=MESH)

    for n in range(3):
        loads[n].wait()
    plume_col = column(plume[...], nl)
    scaled = jnp.where(upw[...] == 1, cour[...], -cour[...]) * plume_col[None]
    face[0, 0:nl, :] = scaled[0]
    face[1, 0:nl, :] = scaled[1]
    face[2, 0:nl, :] = jnp.broadcast_to(plume_col, (nl, ny))
    for k in range(1, 4):
        @pl.when(lev + k > 3)
        def _():
            face[:, k * nl:(k + 1) * nl, :] = jnp.zeros((3, nl, ny), F32)
            nface[k * nl:(k + 1) * nl, :] = jnp.zeros((nl, ny), F32)
    for n in range(3, 5):
        loads[n].wait()
    masked[0] = ctl[...] * mask[...].astype(F32)

    pl.semaphore_wait(barrier, 11)

    def halo(k):
        return send(face.at[0, pl.ds(0, nl)], nface.at[pl.ds(k * nl, nl)], halo_send.at[k], halo_recv.at[k], lev - k, before)

    def down(k):
        return send(face.at[:, pl.ds(0, nl)], face.at[:, pl.ds(k * nl, nl)], down_send.at[k], down_recv.at[k], lev - k, tile)

    edges = [
        send(masked.at[0], edge.at[0], edge_send.at[0], edge_recv.at[0], lev, after),
        send(masked.at[0], edge.at[1], edge_send.at[1], edge_recv.at[1], lev, before),
    ]
    halo(0).start()
    for k in range(1, 4):
        @pl.when(lev >= k)
        def _():
            halo(k).start()
    for copy in edges:
        copy.start()
    for k in range(1, 4):
        @pl.when(lev >= k)
        def _():
            down(k).start()

    for n in range(5, 11):
        loads[n].wait()
    row_i, lane_i = iota((nb, 128), 0), iota((nb, 128), 1)
    weight_row = pad_row(weight[...], 128)
    weight_col = column(weight_row, nb)
    shifted = jnp.broadcast_to(weight_row, (nb, 128))
    for bit in range(7):
        shifted = jnp.where((row_i >> bit) & 1 == 1, pltpu.roll(shifted, 128 - (1 << bit), 1), shifted)
    mixing = jnp.where(row_i + lane_i < nb, shifted, 0.0) - weight_row - weight_col
    mix_hi, mix_lo = split(jnp.where(lane_i < nb, mixing, 0.0))
    lhs[0:nb, 0:128] = mix_hi
    lhs[0:nb, 128:256] = mix_hi
    lhs[nb:2 * nb, 0:128] = mix_lo
    lhs[nb:2 * nb, 128:256] = jnp.zeros((nb, 128), BF16)

    speed_col = column(pad_row(speed[...], 128), nb)
    profile_col = column(pad_row(profile[...], 128), nb)
    here = pltpu.roll(jnp.broadcast_to(pad_row(factor[...], 128), (8, 128)), lax.rem(128 - lev * nl, 128), 1)[0:1]
    fall = speed_col * jnp.where(iota((1, 128), 1) < total, here, 0.0)
    inverse = 1.0 / (1.0 + fall)
    gain = fall * inverse
    for l in range(nl):
        rb[l] = jnp.broadcast_to(inverse[:, l:l + 1], (nb, 128))
        gb[l] = jnp.broadcast_to(gain[:, l:l + 1], (nb, 128))
    chain = jnp.where(lane_i < nl, 1.0, gain)
    step = 1
    while step < total:
        chain = chain * jnp.where(lane_i >= step, pltpu.roll(chain, step, 1), 1.0)
        step *= 2
    chain = jnp.where(lane_i < nl, 0.0, chain)[:, 0:total]

    masked[1] = pltpu.roll(masked[0], 1, 1)
    masked[2] = pltpu.roll(masked[0], ny - 1, 1)

    def mix_level(l, _):
        bg_copy(l).wait()
        hi, lo = split(bg[l])
        rest = jnp.zeros((128 - nb, ny), BF16)
        both = jnp.dot(lhs[...], jnp.concatenate([hi, rest, lo, rest], axis=0), preferred_element_type=F32)
        amp[l] = weight_col + rate[pl.ds(l, 1), :] * (both[0:nb] + both[nb:2 * nb])
        return 0

    lax.fori_loop(0, nl, mix_level, 0)

    for k in range(1, 4):
        @pl.when(lev + k <= 3)
        def _():
            arrived(face.at[:, pl.ds(k * nl, nl)], down_recv.at[k])
    face_x, face_y = face[0], face[1]
    next_y = pltpu.roll(face_y, ny - 1, 1)
    coef[0] = jnp.maximum(face_y, 0.0)
    coef[1] = -jnp.minimum(next_y, 0.0)
    coef[2] = jnp.maximum(face_x, 0.0)
    coef[3] = face[2] + jnp.minimum(face_x, 0.0) + jnp.minimum(face_y, 0.0) - jnp.maximum(next_y, 0.0)
    for n in range(4):
        quot[n] = dot3(chain, coef[n])

    def rows_of(c):
        return pl.ds(pl.multiple_of(c * chunk, 8), chunk)

    def wide(value):
        return jnp.concatenate([value] * (ny // 128), axis=1)

    def du(i, c):
        return send(kern.at[c, pl.ds(0, 2)], du_in.at[lev], du_send.at[i], du_recv.at[lev], c, tile)

    def self_(i, c):
        return send(kern.at[c, 3], self_in.at[lev], self_send.at[i], self_recv.at[lev], c, tile)

    def left(c):
        return send(kern.at[c, 2], left_in.at[lev], left_send.at[c], left_recv.at[lev], c, before)

    def right(c):
        return send(kern.at[c, 4], right_in.at[lev], right_send.at[c], right_recv.at[lev], c, after)

    profile_wide = jnp.broadcast_to(profile_col, (nb, 128))
    rb[nl] = profile_wide

    def settle(i, _):
        c = lax.rem(lev + 1 + i, 4)
        rows = rows_of(c)
        value = jnp.zeros((chunk, ny), F32)
        sums = [jnp.zeros((chunk, ny), F32) for _ in range(4)]
        for l in range(nl):
            value = amp[l, rows, :] * wide(rb[l, rows, :]) + value * wide(gb[l, rows, :])
            bfield[l, rows, :] = value
            for n in range(4):
                sums[n] = sums[n] + value * coef[n, l:l + 1, :]
        prof = wide(rb[nl, rows, :])
        for n in range(4):
            kern[c, n] = prof * (sums[n] + value * quot[n, rows, :])

        @pl.when(i < 3)
        def _():
            du(i, c).start()
        left(c).start()
        return 0

    lax.fori_loop(0, 4, settle, 0)

    arrived(nface.at[pl.ds(0, nl)], halo_recv.at[0])
    for k in range(1, 4):
        @pl.when(lev + k <= 3)
        def _():
            arrived(nface.at[pl.ds(k * nl, nl)], halo_recv.at[k])
    ncoef[0] = jnp.maximum(nface[...], 0.0)
    ncoef[1] = -jnp.minimum(nface[...], 0.0)
    for n in range(2):
        nquot[n] = dot3(chain, ncoef[n])
    for n in range(2):
        arrived(edge.at[n], edge_recv.at[n])

    def finish(i, t_sum):
        c = lax.rem(lev + 1 + i, 4)
        rows = rows_of(c)
        sums = [jnp.zeros((chunk, ny), F32) for _ in range(2)]
        for l in range(nl):
            value = bfield[l, rows, :]
            for n in range(2):
                sums[n] = sums[n] + value * ncoef[n, l:l + 1, :]
        prof = wide(rb[nl, rows, :])
        value = bfield[nl - 1, rows, :]
        k_self = kern[c, 3] - prof * (sums[0] + value * nquot[0, rows, :])
        k_right = prof * (sums[1] + value * nquot[1, rows, :])
        kern[c, 3] = k_self
        kern[c, 4] = k_right

        @pl.when(i < 3)
        def _():
            self_(i, c).start()
        right(c).start()
        part = (
            masked[0, rows, :] * k_self + edge[0, rows, :] * kern[c, 2] + edge[1, rows, :] * k_right
            + masked[1, rows, :] * kern[c, 0] + masked[2, rows, :] * kern[c, 1]
        )
        for r in range(0, chunk, 8):
            t_sum = t_sum + part[r:r + 8]
        return t_sum

    t_sum = lax.fori_loop(0, 4, finish, jnp.zeros((8, ny), F32))
    t_mine = jnp.sum(t_sum, axis=0, keepdims=True) * scale
    s_mine = t_mine * prec[...] * scale
    t_own[...] = t_mine
    s_own[...] = s_mine

    t_sends = []
    for k in range(4):
        t_sends.append(send(s_own, t_left.at[lev], tx_send.at[k], tx_recv.at[lev], k, after))
        t_sends.append(send(s_own, t_right.at[lev], tx_send.at[4 + k], tx_recv.at[4 + lev], k, before))
    for k in range(1, 4):
        t_sends.append(send(t_own, t_lev.at[k], tl_send.at[k], tl_recv.at[k], lev ^ k, tile))
    for copy in t_sends:
        copy.start()

    totals = [kern[lev, 0], kern[lev, 1], kern[lev, 3]]
    for k in range(1, 4):
        d = lax.rem(lev + k, 4)
        arrived(du_in.at[d], du_recv.at[d])
        totals[0] = totals[0] + du_in[d, 0]
        totals[1] = totals[1] + du_in[d, 1]
    for k in range(1, 4):
        d = lax.rem(lev + k, 4)
        arrived(self_in.at[d], self_recv.at[d])
        totals[2] = totals[2] + self_in[d]
    t_all = t_mine
    for k in range(1, 4):
        arrived(t_lev.at[k], tl_recv.at[k])
        t_all = t_all + t_lev[k]
    obs_out[...] = t_all
    s_here = t_all * prec[...] * scale
    result = totals[2] * s_here + pltpu.roll(totals[0] * s_here, ny - 1, 1) + pltpu.roll(totals[1] * s_here, 1, 1)
    for k in range(4):
        arrived(left_in.at[k], left_recv.at[k])
        arrived(right_in.at[k], right_recv.at[k])
    from_after = (left_in[0] + left_in[1]) + (left_in[2] + left_in[3])
    from_before = (right_in[0] + right_in[1]) + (right_in[2] + right_in[3])
    for k in range(4):
        arrived(t_left.at[k], tx_recv.at[k])
        arrived(t_right.at[k], tx_recv.at[4 + k])
    s_before = (t_left[0] + t_left[1]) + (t_left[2] + t_left[3])
    s_after = (t_right[0] + t_right[1]) + (t_right[2] + t_right[3])
    result = mask[...].astype(F32) * (result + from_after * s_after + from_before * s_before)

    mine = rows_of(lev)
    out_buf[mine, :] = result
    gathers = [
        send(out_buf.at[mine], out_buf.at[mine], ag_send.at[k], ag_recv.at[lev], lev ^ k, tile) for k in range(1, 4)
    ]
    for copy in gathers:
        copy.start()

    halo(0).wait_send()
    for k in range(1, 4):
        @pl.when(lev >= k)
        def _():
            halo(k).wait_send()
            down(k).wait_send()
    for copy in edges + t_sends:
        copy.wait_send()
    for i in range(4):
        c = lax.rem(lev + 1 + i, 4)
        if i < 3:
            du(i, c).wait_send()
            self_(i, c).wait_send()
        left(c).wait_send()
        right(c).wait_send()

    for k in range(1, 4):
        d = lev ^ k
        arrived(out_buf.at[rows_of(d)], ag_recv.at[d])
    hess_out[...] = out_buf[...]
    for copy in gathers:
        copy.wait_send()


def per_device(
    control, emit_mask, bin_profile, plume_profile, courant, upwind, bin_speed, level_factor, background, coag_rate,
    obs_weight, obs_precision,
):
    nb, nl, _, ny = background.shape
    total = level_factor.shape[0]
    chunk = nb // 4
    vmem, dma = pltpu.VMEM, pltpu.SemaphoreType.DMA
    obs, hess = pl.pallas_call(
        functools.partial(kernel, nb, nl, total, 1.0 / (nb * total)),
        out_shape=(jax.ShapeDtypeStruct((1, ny), F32), jax.ShapeDtypeStruct((nb, ny), F32)),
        in_specs=[pl.BlockSpec(memory_space=pl.ANY)] * 12,
        out_specs=(pl.BlockSpec(memory_space=pltpu.VMEM),) * 2,
        scratch_shapes=[
            vmem((nl, nb, ny), F32),
            vmem((nb, ny), F32),
            vmem((1, ny), jnp.int32),
            vmem((1, nb), F32),
            vmem((1, nl), F32),
            vmem((2, nl, ny), F32),
            vmem((2, nl, ny), jnp.int32),
            vmem((1, nb), F32),
            vmem((1, total), F32),
            vmem((nl, ny), F32),
            vmem((1, nb), F32),
            vmem((1, ny), F32),
            vmem((2 * nb, 256), BF16),
            vmem((nl, nb, ny), F32),
            vmem((nl + 1, nb, 128), F32),
            vmem((nl, nb, 128), F32),
            vmem((nl, nb, ny), F32),
            vmem((3, total, ny), F32),
            vmem((total, ny), F32),
            vmem((4, total, ny), F32),
            vmem((2, total, ny), F32),
            vmem((4, nb, ny), F32),
            vmem((2, nb, ny), F32),
            vmem((3, nb, ny), F32),
            vmem((2, nb, ny), F32),
            vmem((4, 5, chunk, ny), F32),
            vmem((4, 2, chunk, ny), F32),
            vmem((4, chunk, ny), F32),
            vmem((4, chunk, ny), F32),
            vmem((4, chunk, ny), F32),
            vmem((4, 1, ny), F32),
            vmem((4, 1, ny), F32),
            vmem((4, 1, ny), F32),
            vmem((1, ny), F32),
            vmem((1, ny), F32),
            vmem((nb, ny), F32),
            dma((11,)), dma((nl,)),
            dma((4,)), dma((4,)), dma((4,)), dma((4,)), dma((2,)), dma((2,)),
            dma((4,)), dma((4,)), dma((4,)), dma((4,)), dma((4,)), dma((4,)), dma((4,)), dma((4,)),
            dma((4,)), dma((4,)), dma((8,)), dma((8,)), dma((4,)), dma((4,)),
        ],
        compiler_params=pltpu.CompilerParams(collective_id=0, has_side_effects=True, vmem_limit_bytes=48 << 20),
        name="hessian",
    )(
        control, emit_mask, bin_profile[None], plume_profile[None], courant, upwind, bin_speed[None], level_factor[None],
        background, coag_rate, obs_weight[None], obs_precision,
    )
    return obs, hess[:, None, :]


def solution(mesh):
    in_specs = (
        P(None, "tile", None), P("tile", None), P(), P("lev"), P(None, "lev", "tile", None), P(None, "lev", "tile", None),
        P(), P(), P(None, "lev", "tile", None), P("lev", "tile", None), P(), P("tile", None),
    )
    out_specs = (P("tile", None), P(None, "tile", None))
    return jax.shard_map(per_device, mesh=mesh, in_specs=in_specs, out_specs=out_specs, check_vma=False)
```

```python
import functools

import jax
import jax.numpy as jnp
from jax import lax
from jax.experimental import pallas as pl
from jax.experimental.pallas import tpu as pltpu
from jax.sharding import PartitionSpec as P

MESH = pl.DeviceIdType.MESH
F32, BF16 = jnp.float32, jnp.bfloat16


def split(value):
    high = value.astype(BF16)
    return high, (value - high.astype(F32)).astype(BF16)


def dot3(a, b):
    a_hi, a_lo = split(a)
    b_hi, b_lo = split(b)
    dot = functools.partial(jnp.dot, preferred_element_type=F32)
    return dot(a_hi, b_hi) + (dot(a_hi, b_lo) + dot(a_lo, b_hi))


def iota(shape, dim):
    return lax.broadcasted_iota(jnp.int32, shape, dim)


def pad_row(row, lanes):
    return jnp.concatenate([row, jnp.zeros((1, lanes - row.shape[1]), row.dtype)], axis=1)


def column(row, rows):
    shape = (rows, row.shape[1])
    picked = jnp.where(iota(shape, 0) == iota(shape, 1), jnp.broadcast_to(row, shape), 0.0)
    return jnp.sum(picked, axis=1, keepdims=True)


def kernel(
    nb, nl, total, scale,
    control, mask_in, profile_in, plume_in, courant, upwind, speed_in, factor_in, background, rate_in, weight_in, prec_in,
    obs_out, hess_out,
    bg, ctl, mask, profile, plume, cour, upw, speed, factor, rate, weight, prec,
    lhs, amp, rb, gb, bfield, face, nface, coef, ncoef, quot, nquot, masked, edge, kern,
    du_in, self_in, left_in, right_in, t_lev, t_left, t_right, t_own, s_own, out_buf,
    load_sem, bg_sem,
    halo_send, halo_recv, down_send, down_recv, edge_send, edge_recv,
    du_send, du_recv, self_send, self_recv, left_send, left_recv, right_send, right_recv,
    tl_send, tl_recv, tx_send, tx_recv, ag_send, ag_recv,
):
    lev, tile = lax.axis_index("lev"), lax.axis_index("tile")
    tiles = lax.axis_size("tile")
    before, after = lax.rem(tile + tiles - 1, tiles), lax.rem(tile + 1, tiles)
    ny = bg.shape[2]
    chunk = nb // 4

    def at(lev_to, tile_to):
        return {"lev": lev_to, "tile": tile_to}

    def send(src, dst, send_sem, recv_sem, lev_to, tile_to):
        return pltpu.make_async_remote_copy(
            src_ref=src, dst_ref=dst, send_sem=send_sem, recv_sem=recv_sem,
            device_id=at(lev_to, tile_to), device_id_type=MESH,
        )

    def arrived(dst, sem):
        pltpu.make_async_copy(dst, dst, sem).wait()

    barrier = pltpu.get_barrier_semaphore()
    for near in (before, after):
        for k in range(4):
            pl.semaphore_signal(barrier, inc=1, device_id=at(k, near), device_id_type=MESH)
    for k in range(1, 4):
        pl.semaphore_signal(barrier, inc=1, device_id=at(lev ^ k, tile), device_id_type=MESH)

    small = [
        (courant.at[:, :, 0, :], cour), (upwind.at[:, :, 0, :], upw), (plume_in, plume), (control.at[:, 0, :], ctl),
        (mask_in, mask), (speed_in, speed), (factor_in, factor), (weight_in, weight), (profile_in, profile),
        (rate_in.at[:, 0, :], rate), (prec_in, prec),
    ]
    loads = [pltpu.make_async_copy(a, b, load_sem.at[n]) for n, (a, b) in enumerate(small)]
    for copy in loads:
        copy.start()

    def bg_copy(l):
        return pltpu.make_async_copy(background.at[:, l, 0, :], bg.at[l], bg_sem.at[l])

    def bg_start(l, _):
        bg_copy(l).start()
        return 0

    lax.fori_loop(0, nl, bg_start, 0)

    for n in range(3):
        loads[n].wait()
    plume_col = column(plume[...], nl)
    scaled = jnp.where(upw[...] == 1, cour[...], -cour[...]) * plume_col[None]
    face[0, 0:nl, :] = scaled[0]
    face[1, 0:nl, :] = scaled[1]
    face[2, 0:nl, :] = jnp.broadcast_to(plume_col, (nl, ny))
    for k in range(1, 4):
        @pl.when(lev + k > 3)
        def _():
            face[:, k * nl:(k + 1) * nl, :] = jnp.zeros((3, nl, ny), F32)
            nface[k * nl:(k + 1) * nl, :] = jnp.zeros((nl, ny), F32)
    for n in range(3, 5):
        loads[n].wait()
    masked[0] = ctl[...] * mask[...].astype(F32)

    pl.semaphore_wait(barrier, 11)

    def halo(k):
        return send(face.at[0, pl.ds(0, nl)], nface.at[pl.ds(k * nl, nl)], halo_send.at[k], halo_recv.at[k], lev - k, before)

    def down(k):
        return send(face.at[:, pl.ds(0, nl)], face.at[:, pl.ds(k * nl, nl)], down_send.at[k], down_recv.at[k], lev - k, tile)

    edges = [
        send(masked.at[0], edge.at[0], edge_send.at[0], edge_recv.at[0], lev, after),
        send(masked.at[0], edge.at[1], edge_send.at[1], edge_recv.at[1], lev, before),
    ]
    halo(0).start()
    for k in range(1, 4):
        @pl.when(lev >= k)
        def _():
            halo(k).start()
    for copy in edges:
        copy.start()
    for k in range(1, 4):
        @pl.when(lev >= k)
        def _():
            down(k).start()

    for n in range(5, 11):
        loads[n].wait()
    row_i, lane_i = iota((nb, 128), 0), iota((nb, 128), 1)
    weight_row = pad_row(weight[...], 128)
    weight_col = column(weight_row, nb)
    shifted = jnp.broadcast_to(weight_row, (nb, 128))
    for bit in range(7):
        shifted = jnp.where((row_i >> bit) & 1 == 1, pltpu.roll(shifted, 128 - (1 << bit), 1), shifted)
    mixing = jnp.where(row_i + lane_i < nb, shifted, 0.0) - weight_row - weight_col
    mix_hi, mix_lo = split(jnp.where(lane_i < nb, mixing, 0.0))
    lhs[0:nb, 0:128] = mix_hi
    lhs[0:nb, 128:256] = mix_hi
    lhs[nb:2 * nb, 0:128] = mix_lo
    lhs[nb:2 * nb, 128:256] = jnp.zeros((nb, 128), BF16)

    speed_col = column(pad_row(speed[...], 128), nb)
    profile_col = column(pad_row(profile[...], 128), nb)
    here = pltpu.roll(jnp.broadcast_to(pad_row(factor[...], 128), (8, 128)), lax.rem(128 - lev * nl, 128), 1)[0:1]
    fall = speed_col * jnp.where(iota((1, 128), 1) < total, here, 0.0)
    inverse = 1.0 / (1.0 + fall)
    gain = fall * inverse
    for l in range(nl):
        rb[l] = jnp.broadcast_to(inverse[:, l:l + 1], (nb, 128))
        gb[l] = jnp.broadcast_to(gain[:, l:l + 1], (nb, 128))
    chain = jnp.where(lane_i < nl, 1.0, gain)
    step = 1
    while step < total:
        chain = chain * jnp.where(lane_i >= step, pltpu.roll(chain, step, 1), 1.0)
        step *= 2
    chain = jnp.where(lane_i < nl, 0.0, chain)[:, 0:total]

    masked[1] = pltpu.roll(masked[0], 1, 1)
    masked[2] = pltpu.roll(masked[0], ny - 1, 1)

    def mix_level(l, _):
        bg_copy(l).wait()
        hi, lo = split(bg[l])
        rest = jnp.zeros((128 - nb, ny), BF16)
        both = jnp.dot(lhs[...], jnp.concatenate([hi, rest, lo, rest], axis=0), preferred_element_type=F32)
        amp[l] = weight_col + rate[pl.ds(l, 1), :] * (both[0:nb] + both[nb:2 * nb])
        return 0

    lax.fori_loop(0, nl, mix_level, 0)

    for k in range(1, 4):
        @pl.when(lev + k <= 3)
        def _():
            arrived(face.at[:, pl.ds(k * nl, nl)], down_recv.at[k])
    face_x, face_y = face[0], face[1]
    next_y = pltpu.roll(face_y, ny - 1, 1)
    coef[0] = jnp.maximum(face_y, 0.0)
    coef[1] = -jnp.minimum(next_y, 0.0)
    coef[2] = jnp.maximum(face_x, 0.0)
    coef[3] = face[2] + jnp.minimum(face_x, 0.0) + jnp.minimum(face_y, 0.0) - jnp.maximum(next_y, 0.0)
    for n in range(4):
        quot[n] = dot3(chain, coef[n])

    def rows_of(c):
        return pl.ds(pl.multiple_of(c * chunk, 8), chunk)

    def wide(value):
        return jnp.concatenate([value] * (ny // 128), axis=1)

    def du(i, c):
        return send(kern.at[c, pl.ds(0, 2)], du_in.at[lev], du_send.at[i], du_recv.at[lev], c, tile)

    def self_(i, c):
        return send(kern.at[c, 3], self_in.at[lev], self_send.at[i], self_recv.at[lev], c, tile)

    def left(c):
        return send(kern.at[c, 2], left_in.at[lev], left_send.at[c], left_recv.at[lev], c, before)

    def right(c):
        return send(kern.at[c, 4], right_in.at[lev], right_send.at[c], right_recv.at[lev], c, after)

    profile_wide = jnp.broadcast_to(profile_col, (nb, 128))
    rb[nl] = profile_wide

    def settle(i, _):
        c = lax.rem(lev + 1 + i, 4)
        rows = rows_of(c)
        value = jnp.zeros((chunk, ny), F32)
        sums = [jnp.zeros((chunk, ny), F32) for _ in range(4)]
        for l in range(nl):
            value = amp[l, rows, :] * wide(rb[l, rows, :]) + value * wide(gb[l, rows, :])
            bfield[l, rows, :] = value
            for n in range(4):
                sums[n] = sums[n] + value * coef[n, l:l + 1, :]
        prof = wide(rb[nl, rows, :])
        for n in range(4):
            kern[c, n] = prof * (sums[n] + value * quot[n, rows, :])

        @pl.when(i < 3)
        def _():
            du(i, c).start()
        left(c).start()
        return 0

    lax.fori_loop(0, 4, settle, 0)

    arrived(nface.at[pl.ds(0, nl)], halo_recv.at[0])
    for k in range(1, 4):
        @pl.when(lev + k <= 3)
        def _():
            arrived(nface.at[pl.ds(k * nl, nl)], halo_recv.at[k])
    ncoef[0] = jnp.maximum(nface[...], 0.0)
    ncoef[1] = -jnp.minimum(nface[...], 0.0)
    for n in range(2):
        nquot[n] = dot3(chain, ncoef[n])
    for n in range(2):
        arrived(edge.at[n], edge_recv.at[n])

    def finish(i, t_sum):
        c = lax.rem(lev + 1 + i, 4)
        rows = rows_of(c)
        sums = [jnp.zeros((chunk, ny), F32) for _ in range(2)]
        for l in range(nl):
            value = bfield[l, rows, :]
            for n in range(2):
                sums[n] = sums[n] + value * ncoef[n, l:l + 1, :]
        prof = wide(rb[nl, rows, :])
        value = bfield[nl - 1, rows, :]
        k_self = kern[c, 3] - prof * (sums[0] + value * nquot[0, rows, :])
        k_right = prof * (sums[1] + value * nquot[1, rows, :])
        kern[c, 3] = k_self
        kern[c, 4] = k_right

        @pl.when(i < 3)
        def _():
            self_(i, c).start()
        right(c).start()
        part = (
            masked[0, rows, :] * k_self + edge[0, rows, :] * kern[c, 2] + edge[1, rows, :] * k_right
            + masked[1, rows, :] * kern[c, 0] + masked[2, rows, :] * kern[c, 1]
        )
        for r in range(0, chunk, 8):
            t_sum = t_sum + part[r:r + 8]
        return t_sum

    t_sum = lax.fori_loop(0, 4, finish, jnp.zeros((8, ny), F32))
    t_mine = jnp.sum(t_sum, axis=0, keepdims=True) * scale
    s_mine = t_mine * prec[...] * scale
    t_own[...] = t_mine
    s_own[...] = s_mine

    t_sends = []
    for k in range(4):
        t_sends.append(send(s_own, t_left.at[lev], tx_send.at[k], tx_recv.at[lev], k, after))
        t_sends.append(send(s_own, t_right.at[lev], tx_send.at[4 + k], tx_recv.at[4 + lev], k, before))
    for k in range(1, 4):
        t_sends.append(send(t_own, t_lev.at[k], tl_send.at[k], tl_recv.at[k], lev ^ k, tile))
    for copy in t_sends:
        copy.start()

    totals = [kern[lev, 0], kern[lev, 1], kern[lev, 3]]
    for k in range(1, 4):
        d = lax.rem(lev + k, 4)
        arrived(du_in.at[d], du_recv.at[d])
        totals[0] = totals[0] + du_in[d, 0]
        totals[1] = totals[1] + du_in[d, 1]
    for k in range(1, 4):
        d = lax.rem(lev + k, 4)
        arrived(self_in.at[d], self_recv.at[d])
        totals[2] = totals[2] + self_in[d]
    t_all = t_mine
    for k in range(1, 4):
        arrived(t_lev.at[k], tl_recv.at[k])
        t_all = t_all + t_lev[k]
    obs_out[...] = t_all
    s_here = t_all * prec[...] * scale
    result = totals[2] * s_here + pltpu.roll(totals[0] * s_here, ny - 1, 1) + pltpu.roll(totals[1] * s_here, 1, 1)
    for k in range(4):
        arrived(left_in.at[k], left_recv.at[k])
        arrived(right_in.at[k], right_recv.at[k])
    from_after = (left_in[0] + left_in[1]) + (left_in[2] + left_in[3])
    from_before = (right_in[0] + right_in[1]) + (right_in[2] + right_in[3])
    for k in range(4):
        arrived(t_left.at[k], tx_recv.at[k])
        arrived(t_right.at[k], tx_recv.at[4 + k])
    s_before = (t_left[0] + t_left[1]) + (t_left[2] + t_left[3])
    s_after = (t_right[0] + t_right[1]) + (t_right[2] + t_right[3])
    result = mask[...].astype(F32) * (result + from_after * s_after + from_before * s_before)

    mine = rows_of(lev)
    out_buf[mine, :] = result
    gathers = [
        send(out_buf.at[mine], out_buf.at[mine], ag_send.at[k], ag_recv.at[lev], lev ^ k, tile) for k in range(1, 4)
    ]
    for copy in gathers:
        copy.start()

    halo(0).wait_send()
    for k in range(1, 4):
        @pl.when(lev >= k)
        def _():
            halo(k).wait_send()
            down(k).wait_send()
    for copy in edges + t_sends:
        copy.wait_send()
    for i in range(4):
        c = lax.rem(lev + 1 + i, 4)
        if i < 3:
            du(i, c).wait_send()
            self_(i, c).wait_send()
        left(c).wait_send()
        right(c).wait_send()

    for k in range(1, 4):
        d = lev ^ k
        arrived(out_buf.at[rows_of(d)], ag_recv.at[d])
    hess_out[...] = out_buf[...]
    for copy in gathers:
        copy.wait_send()


def per_device(
    control, emit_mask, bin_profile, plume_profile, courant, upwind, bin_speed, level_factor, background, coag_rate,
    obs_weight, obs_precision,
):
    nb, nl, _, ny = background.shape
    total = level_factor.shape[0]
    chunk = nb // 4
    vmem, dma = pltpu.VMEM, pltpu.SemaphoreType.DMA
    obs, hess = pl.pallas_call(
        functools.partial(kernel, nb, nl, total, 1.0 / (nb * total)),
        out_shape=(jax.ShapeDtypeStruct((1, ny), F32), jax.ShapeDtypeStruct((nb, ny), F32)),
        in_specs=[pl.BlockSpec(memory_space=pl.ANY)] * 12,
        out_specs=(pl.BlockSpec(memory_space=pltpu.VMEM),) * 2,
        scratch_shapes=[
            vmem((nl, nb, ny), F32),
            vmem((nb, ny), F32),
            vmem((1, ny), jnp.int32),
            vmem((1, nb), F32),
            vmem((1, nl), F32),
            vmem((2, nl, ny), F32),
            vmem((2, nl, ny), jnp.int32),
            vmem((1, nb), F32),
            vmem((1, total), F32),
            vmem((nl, ny), F32),
            vmem((1, nb), F32),
            vmem((1, ny), F32),
            vmem((2 * nb, 256), BF16),
            vmem((nl, nb, ny), F32),
            vmem((nl + 1, nb, 128), F32),
            vmem((nl, nb, 128), F32),
            vmem((nl, nb, ny), F32),
            vmem((3, total, ny), F32),
            vmem((total, ny), F32),
            vmem((4, total, ny), F32),
            vmem((2, total, ny), F32),
            vmem((4, nb, ny), F32),
            vmem((2, nb, ny), F32),
            vmem((3, nb, ny), F32),
            vmem((2, nb, ny), F32),
            vmem((4, 5, chunk, ny), F32),
            vmem((4, 2, chunk, ny), F32),
            vmem((4, chunk, ny), F32),
            vmem((4, chunk, ny), F32),
            vmem((4, chunk, ny), F32),
            vmem((4, 1, ny), F32),
            vmem((4, 1, ny), F32),
            vmem((4, 1, ny), F32),
            vmem((1, ny), F32),
            vmem((1, ny), F32),
            vmem((nb, ny), F32),
            dma((11,)), dma((nl,)),
            dma((4,)), dma((4,)), dma((4,)), dma((4,)), dma((2,)), dma((2,)),
            dma((4,)), dma((4,)), dma((4,)), dma((4,)), dma((4,)), dma((4,)), dma((4,)), dma((4,)),
            dma((4,)), dma((4,)), dma((8,)), dma((8,)), dma((4,)), dma((4,)),
        ],
        compiler_params=pltpu.CompilerParams(collective_id=0, has_side_effects=True, vmem_limit_bytes=24 << 20),
        name="hessian",
    )(*[
        pltpu.with_memory_space_constraint(value, pltpu.HBM) for value in (
            control, emit_mask, bin_profile[None], plume_profile[None], courant, upwind, bin_speed[None],
            level_factor[None], background, coag_rate, obs_weight[None], obs_precision,
        )
    ])
    return obs, hess[:, None, :]


def solution(mesh):
    in_specs = (
        P(None, "tile", None), P("tile", None), P(), P("lev"), P(None, "lev", "tile", None), P(None, "lev", "tile", None),
        P(), P(), P(None, "lev", "tile", None), P("lev", "tile", None), P(), P("tile", None),
    )
    out_specs = (P("tile", None), P(None, "tile", None))
    return jax.shard_map(per_device, mesh=mesh, in_specs=in_specs, out_specs=out_specs, check_vma=False)
```

```python
import functools

import jax
import jax.numpy as jnp
from jax import lax
from jax.experimental import pallas as pl
from jax.experimental.pallas import tpu as pltpu
from jax.sharding import PartitionSpec as P

MESH = pl.DeviceIdType.MESH
F32, BF16 = jnp.float32, jnp.bfloat16


def split(value):
    high = value.astype(BF16)
    return high, (value - high.astype(F32)).astype(BF16)


def dot3(a, b):
    a_hi, a_lo = split(a)
    b_hi, b_lo = split(b)
    dot = functools.partial(jnp.dot, preferred_element_type=F32)
    return dot(a_hi, b_hi) + (dot(a_hi, b_lo) + dot(a_lo, b_hi))


def iota(shape, dim):
    return lax.broadcasted_iota(jnp.int32, shape, dim)


def pad_row(row, lanes):
    return jnp.concatenate([row, jnp.zeros((1, lanes - row.shape[1]), row.dtype)], axis=1)


def column(row, rows):
    shape = (rows, row.shape[1])
    picked = jnp.where(iota(shape, 0) == iota(shape, 1), jnp.broadcast_to(row, shape), 0.0)
    return jnp.sum(picked, axis=1, keepdims=True)


def kernel(
    nb, nl, total, scale,
    control, mask_in, profile_in, plume_in, courant, upwind, speed_in, factor_in, background, rate_in, weight_in, prec_in,
    obs_out, hess_out,
    bg, ctl, mask, profile, plume, cour, upw, speed, factor, rate, weight, prec,
    lhs, amp, rb, gb, bfield, face, nface, coef, ncoef, quot, nquot, masked, edge, kern,
    du_in, self_in, left_in, right_in, t_lev, t_left, t_right, t_own, s_own, out_buf,
    load_sem, bg_sem,
    halo_send, halo_recv, down_send, down_recv, edge_send, edge_recv,
    du_send, du_recv, self_send, self_recv, left_send, left_recv, right_send, right_recv,
    tl_send, tl_recv, tx_send, tx_recv, ag_send, ag_recv,
):
    lev, tile = lax.axis_index("lev"), lax.axis_index("tile")
    tiles = lax.axis_size("tile")
    before, after = lax.rem(tile + tiles - 1, tiles), lax.rem(tile + 1, tiles)
    ny = bg.shape[2]
    chunk = nb // 4

    def at(lev_to, tile_to):
        return {"lev": lev_to, "tile": tile_to}

    def send(src, dst, send_sem, recv_sem, lev_to, tile_to):
        return pltpu.make_async_remote_copy(
            src_ref=src, dst_ref=dst, send_sem=send_sem, recv_sem=recv_sem,
            device_id=at(lev_to, tile_to), device_id_type=MESH,
        )

    def arrived(dst, sem):
        pltpu.make_async_copy(dst, dst, sem).wait()

    barrier = pltpu.get_barrier_semaphore()
    for near in (before, after):
        for k in range(4):
            pl.semaphore_signal(barrier, inc=1, device_id=at(k, near), device_id_type=MESH)
    for k in range(1, 4):
        pl.semaphore_signal(barrier, inc=1, device_id=at(lev ^ k, tile), device_id_type=MESH)

    small = [
        (courant.at[:, :, 0, :], cour), (upwind.at[:, :, 0, :], upw), (plume_in, plume), (control.at[:, 0, :], ctl),
        (mask_in, mask), (speed_in, speed), (factor_in, factor), (weight_in, weight), (profile_in, profile),
        (rate_in.at[:, 0, :], rate), (prec_in, prec),
    ]
    loads = [pltpu.make_async_copy(a, b, load_sem.at[n]) for n, (a, b) in enumerate(small)]
    for copy in loads:
        copy.start()

    def bg_copy(l):
        return pltpu.make_async_copy(background.at[:, l, 0, :], bg.at[l], bg_sem.at[l])

    def bg_start(l, _):
        bg_copy(l).start()
        return 0

    lax.fori_loop(0, nl, bg_start, 0)

    for n in range(3):
        loads[n].wait()
    plume_col = column(plume[...], nl)
    scaled = jnp.where(upw[...] == 1, cour[...], -cour[...]) * plume_col[None]
    face[0, 0:nl, :] = scaled[0]
    face[1, 0:nl, :] = scaled[1]
    face[2, 0:nl, :] = jnp.broadcast_to(plume_col, (nl, ny))
    for k in range(1, 4):
        @pl.when(lev + k > 3)
        def _():
            face[:, k * nl:(k + 1) * nl, :] = jnp.zeros((3, nl, ny), F32)
            nface[k * nl:(k + 1) * nl, :] = jnp.zeros((nl, ny), F32)
    for n in range(3, 5):
        loads[n].wait()
    masked[0] = ctl[...] * mask[...].astype(F32)

    pl.semaphore_wait(barrier, 11)

    def halo(k):
        return send(face.at[0, pl.ds(0, nl)], nface.at[pl.ds(k * nl, nl)], halo_send.at[k], halo_recv.at[k], lev - k, before)

    def down(k):
        return send(face.at[:, pl.ds(0, nl)], face.at[:, pl.ds(k * nl, nl)], down_send.at[k], down_recv.at[k], lev - k, tile)

    lev_after = lev ^ jnp.where(lax.rem(tile, 8) == 7, 2, 0)
    lev_before = lev ^ jnp.where(lax.rem(tile, 8) == 0, 2, 0)
    edges = [
        send(masked.at[0], edge.at[0], edge_send.at[0], edge_recv.at[0], lev_after, after),
        send(masked.at[0], edge.at[1], edge_send.at[1], edge_recv.at[1], lev_before, before),
    ]
    halo(0).start()
    for k in range(1, 4):
        @pl.when(lev >= k)
        def _():
            halo(k).start()
    edges[1].start()
    edges[0].start()
    for k in range(1, 4):
        @pl.when(lev >= k)
        def _():
            down(k).start()

    for n in range(5, 11):
        loads[n].wait()
    row_i, lane_i = iota((nb, 128), 0), iota((nb, 128), 1)
    weight_row = pad_row(weight[...], 128)
    weight_col = column(weight_row, nb)
    shifted = jnp.broadcast_to(weight_row, (nb, 128))
    for bit in range(7):
        shifted = jnp.where((row_i >> bit) & 1 == 1, pltpu.roll(shifted, 128 - (1 << bit), 1), shifted)
    mixing = jnp.where(row_i + lane_i < nb, shifted, 0.0) - weight_row - weight_col
    mix_hi, mix_lo = split(jnp.where(lane_i < nb, mixing, 0.0))
    lhs[0:nb, 0:128] = mix_hi
    lhs[0:nb, 128:256] = mix_hi
    lhs[nb:2 * nb, 0:128] = mix_lo
    lhs[nb:2 * nb, 128:256] = jnp.zeros((nb, 128), BF16)

    speed_col = column(pad_row(speed[...], 128), nb)
    profile_col = column(pad_row(profile[...], 128), nb)
    here = pltpu.roll(jnp.broadcast_to(pad_row(factor[...], 128), (8, 128)), lax.rem(128 - lev * nl, 128), 1)[0:1]
    fall = speed_col * jnp.where(iota((1, 128), 1) < total, here, 0.0)
    inverse = 1.0 / (1.0 + fall)
    gain = fall * inverse
    for l in range(nl):
        rb[l] = jnp.broadcast_to(inverse[:, l:l + 1], (nb, 128))
        gb[l] = jnp.broadcast_to(gain[:, l:l + 1], (nb, 128))
    chain = jnp.where(lane_i < nl, 1.0, gain)
    step = 1
    while step < total:
        chain = chain * jnp.where(lane_i >= step, pltpu.roll(chain, step, 1), 1.0)
        step *= 2
    chain = jnp.where(lane_i < nl, 0.0, chain)[:, 0:total]

    masked[1] = pltpu.roll(masked[0], 1, 1)
    masked[2] = pltpu.roll(masked[0], ny - 1, 1)

    def mix_level(l, _):
        bg_copy(l).wait()
        hi, lo = split(bg[l])
        rest = jnp.zeros((128 - nb, ny), BF16)
        both = jnp.dot(lhs[...], jnp.concatenate([hi, rest, lo, rest], axis=0), preferred_element_type=F32)
        amp[l] = weight_col + rate[pl.ds(l, 1), :] * (both[0:nb] + both[nb:2 * nb])
        return 0

    lax.fori_loop(0, nl, mix_level, 0)

    for k in range(1, 4):
        @pl.when(lev + k <= 3)
        def _():
            arrived(face.at[:, pl.ds(k * nl, nl)], down_recv.at[k])
    face_x, face_y = face[0], face[1]
    next_y = pltpu.roll(face_y, ny - 1, 1)
    coef[0] = jnp.maximum(face_y, 0.0)
    coef[1] = -jnp.minimum(next_y, 0.0)
    coef[2] = jnp.maximum(face_x, 0.0)
    coef[3] = face[2] + jnp.minimum(face_x, 0.0) + jnp.minimum(face_y, 0.0) - jnp.maximum(next_y, 0.0)
    for n in range(4):
        quot[n] = dot3(chain, coef[n])

    def rows_of(c):
        return pl.ds(pl.multiple_of(c * chunk, 8), chunk)

    def wide(value):
        return jnp.concatenate([value] * (ny // 128), axis=1)

    def du(i, c):
        return send(kern.at[c, pl.ds(0, 2)], du_in.at[lev], du_send.at[i], du_recv.at[lev], c, tile)

    def self_(i, c):
        return send(kern.at[c, 3], self_in.at[lev], self_send.at[i], self_recv.at[lev], c, tile)

    def left(c):
        return send(kern.at[c, 2], left_in.at[lev], left_send.at[c], left_recv.at[lev], c, before)

    def right(c):
        return send(kern.at[c, 4], right_in.at[lev], right_send.at[c], right_recv.at[lev], c, after)

    profile_wide = jnp.broadcast_to(profile_col, (nb, 128))
    rb[nl] = profile_wide

    def settle(i, _):
        c = lax.rem(lev + 1 + i, 4)
        rows = rows_of(c)
        value = jnp.zeros((chunk, ny), F32)
        sums = [jnp.zeros((chunk, ny), F32) for _ in range(4)]
        for l in range(nl):
            value = amp[l, rows, :] * wide(rb[l, rows, :]) + value * wide(gb[l, rows, :])
            bfield[l, rows, :] = value
            for n in range(4):
                sums[n] = sums[n] + value * coef[n, l:l + 1, :]
        prof = wide(rb[nl, rows, :])
        for n in range(4):
            kern[c, n] = prof * (sums[n] + value * quot[n, rows, :])

        @pl.when(i < 3)
        def _():
            du(i, c).start()
        left(c).start()
        return 0

    lax.fori_loop(0, 4, settle, 0)

    arrived(nface.at[pl.ds(0, nl)], halo_recv.at[0])
    for k in range(1, 4):
        @pl.when(lev + k <= 3)
        def _():
            arrived(nface.at[pl.ds(k * nl, nl)], halo_recv.at[k])
    ncoef[0] = jnp.maximum(nface[...], 0.0)
    ncoef[1] = -jnp.minimum(nface[...], 0.0)
    for n in range(2):
        nquot[n] = dot3(chain, ncoef[n])

    def finish(i, t_sum):
        c = lax.rem(lev + 1 + i, 4)
        rows = rows_of(c)
        sums = [jnp.zeros((chunk, ny), F32) for _ in range(2)]
        for l in range(nl):
            value = bfield[l, rows, :]
            for n in range(2):
                sums[n] = sums[n] + value * ncoef[n, l:l + 1, :]
        prof = wide(rb[nl, rows, :])
        value = bfield[nl - 1, rows, :]
        k_self = kern[c, 3] - prof * (sums[0] + value * nquot[0, rows, :])
        k_right = prof * (sums[1] + value * nquot[1, rows, :])
        kern[c, 3] = k_self
        kern[c, 4] = k_right

        @pl.when(i < 3)
        def _():
            self_(i, c).start()
        right(c).start()
        part = masked[0, rows, :] * k_self + masked[1, rows, :] * kern[c, 0] + masked[2, rows, :] * kern[c, 1]
        for r in range(0, chunk, 8):
            t_sum = t_sum + part[r:r + 8]
        return t_sum

    t_sum = lax.fori_loop(0, 4, finish, jnp.zeros((8, ny), F32))
    for n in range(2):
        arrived(edge.at[n], edge_recv.at[n])
    for c in range(4):
        rows = pl.ds(c * chunk, chunk)
        part = edge[0, rows, :] * kern[c, 2] + edge[1, rows, :] * kern[c, 4]
        for r in range(0, chunk, 8):
            t_sum = t_sum + part[r:r + 8]
    t_mine = jnp.sum(t_sum, axis=0, keepdims=True) * scale
    s_mine = t_mine * prec[...] * scale
    t_own[...] = t_mine
    s_own[...] = s_mine

    t_sends = []
    for k in range(4):
        t_sends.append(send(s_own, t_left.at[lev], tx_send.at[k], tx_recv.at[lev], k, after))
        t_sends.append(send(s_own, t_right.at[lev], tx_send.at[4 + k], tx_recv.at[4 + lev], k, before))
    for k in range(1, 4):
        t_sends.append(send(t_own, t_lev.at[k], tl_send.at[k], tl_recv.at[k], lev ^ k, tile))
    for copy in t_sends:
        copy.start()

    totals = [kern[lev, 0], kern[lev, 1], kern[lev, 3]]
    for k in range(1, 4):
        d = lax.rem(lev + k, 4)
        arrived(du_in.at[d], du_recv.at[d])
        totals[0] = totals[0] + du_in[d, 0]
        totals[1] = totals[1] + du_in[d, 1]
    for k in range(1, 4):
        d = lax.rem(lev + k, 4)
        arrived(self_in.at[d], self_recv.at[d])
        totals[2] = totals[2] + self_in[d]
    t_all = t_mine
    for k in range(1, 4):
        arrived(t_lev.at[k], tl_recv.at[k])
        t_all = t_all + t_lev[k]
    obs_out[...] = t_all
    s_here = t_all * prec[...] * scale
    result = totals[2] * s_here + pltpu.roll(totals[0] * s_here, ny - 1, 1) + pltpu.roll(totals[1] * s_here, 1, 1)
    for k in range(4):
        arrived(left_in.at[k], left_recv.at[k])
        arrived(right_in.at[k], right_recv.at[k])
    from_after = (left_in[0] + left_in[1]) + (left_in[2] + left_in[3])
    from_before = (right_in[0] + right_in[1]) + (right_in[2] + right_in[3])
    for k in range(4):
        arrived(t_left.at[k], tx_recv.at[k])
        arrived(t_right.at[k], tx_recv.at[4 + k])
    s_before = (t_left[0] + t_left[1]) + (t_left[2] + t_left[3])
    s_after = (t_right[0] + t_right[1]) + (t_right[2] + t_right[3])
    result = mask[...].astype(F32) * (result + from_after * s_after + from_before * s_before)

    mine = rows_of(lev)
    out_buf[mine, :] = result
    gathers = [
        send(out_buf.at[mine], out_buf.at[mine], ag_send.at[k], ag_recv.at[lev], lev ^ k, tile) for k in range(1, 4)
    ]
    for copy in gathers:
        copy.start()

    halo(0).wait_send()
    for k in range(1, 4):
        @pl.when(lev >= k)
        def _():
            halo(k).wait_send()
            down(k).wait_send()
    for copy in edges + t_sends:
        copy.wait_send()
    for i in range(4):
        c = lax.rem(lev + 1 + i, 4)
        if i < 3:
            du(i, c).wait_send()
            self_(i, c).wait_send()
        left(c).wait_send()
        right(c).wait_send()

    for k in range(1, 4):
        d = lev ^ k
        arrived(out_buf.at[rows_of(d)], ag_recv.at[d])
    hess_out[...] = out_buf[...]
    for copy in gathers:
        copy.wait_send()


def per_device(
    control, emit_mask, bin_profile, plume_profile, courant, upwind, bin_speed, level_factor, background, coag_rate,
    obs_weight, obs_precision,
):
    nb, nl, _, ny = background.shape
    total = level_factor.shape[0]
    chunk = nb // 4
    vmem, dma = pltpu.VMEM, pltpu.SemaphoreType.DMA
    obs, hess = pl.pallas_call(
        functools.partial(kernel, nb, nl, total, 1.0 / (nb * total)),
        out_shape=(jax.ShapeDtypeStruct((1, ny), F32), jax.ShapeDtypeStruct((nb, ny), F32)),
        in_specs=[pl.BlockSpec(memory_space=pl.ANY)] * 12,
        out_specs=(pl.BlockSpec(memory_space=pltpu.VMEM),) * 2,
        scratch_shapes=[
            vmem((nl, nb, ny), F32),
            vmem((nb, ny), F32),
            vmem((1, ny), jnp.int32),
            vmem((1, nb), F32),
            vmem((1, nl), F32),
            vmem((2, nl, ny), F32),
            vmem((2, nl, ny), jnp.int32),
            vmem((1, nb), F32),
            vmem((1, total), F32),
            vmem((nl, ny), F32),
            vmem((1, nb), F32),
            vmem((1, ny), F32),
            vmem((2 * nb, 256), BF16),
            vmem((nl, nb, ny), F32),
            vmem((nl + 1, nb, 128), F32),
            vmem((nl, nb, 128), F32),
            vmem((nl, nb, ny), F32),
            vmem((3, total, ny), F32),
            vmem((total, ny), F32),
            vmem((4, total, ny), F32),
            vmem((2, total, ny), F32),
            vmem((4, nb, ny), F32),
            vmem((2, nb, ny), F32),
            vmem((3, nb, ny), F32),
            vmem((2, nb, ny), F32),
            vmem((4, 5, chunk, ny), F32),
            vmem((4, 2, chunk, ny), F32),
            vmem((4, chunk, ny), F32),
            vmem((4, chunk, ny), F32),
            vmem((4, chunk, ny), F32),
            vmem((4, 1, ny), F32),
            vmem((4, 1, ny), F32),
            vmem((4, 1, ny), F32),
            vmem((1, ny), F32),
            vmem((1, ny), F32),
            vmem((nb, ny), F32),
            dma((11,)), dma((nl,)),
            dma((4,)), dma((4,)), dma((4,)), dma((4,)), dma((2,)), dma((2,)),
            dma((4,)), dma((4,)), dma((4,)), dma((4,)), dma((4,)), dma((4,)), dma((4,)), dma((4,)),
            dma((4,)), dma((4,)), dma((8,)), dma((8,)), dma((4,)), dma((4,)),
        ],
        compiler_params=pltpu.CompilerParams(collective_id=0, has_side_effects=True, vmem_limit_bytes=24 << 20),
        name="hessian",
    )(*[
        pltpu.with_memory_space_constraint(value, pltpu.HBM) for value in (
            control, emit_mask, bin_profile[None], plume_profile[None], courant, upwind, bin_speed[None],
            level_factor[None], background, coag_rate, obs_weight[None], obs_precision,
        )
    ])
    return obs, hess[:, None, :]


def solution(mesh):
    in_specs = (
        P(None, "tile", None), P("tile", None), P(), P("lev"), P(None, "lev", "tile", None), P(None, "lev", "tile", None),
        P(), P(), P(None, "lev", "tile", None), P("lev", "tile", None), P(), P("tile", None),
    )
    out_specs = (P("tile", None), P(None, "tile", None))
    return jax.shard_map(per_device, mesh=mesh, in_specs=in_specs, out_specs=out_specs, check_vma=False)
```

```python
import functools

import jax
import jax.numpy as jnp
from jax import lax
from jax.experimental import pallas as pl
from jax.experimental.pallas import tpu as pltpu
from jax.sharding import PartitionSpec as P

MESH = pl.DeviceIdType.MESH
F32, BF16 = jnp.float32, jnp.bfloat16


def split(value):
    high = value.astype(BF16)
    return high, (value - high.astype(F32)).astype(BF16)


def dot3(a, b):
    a_hi, a_lo = split(a)
    b_hi, b_lo = split(b)
    dot = functools.partial(jnp.dot, preferred_element_type=F32)
    return dot(a_hi, b_hi) + (dot(a_hi, b_lo) + dot(a_lo, b_hi))


def iota(shape, dim):
    return lax.broadcasted_iota(jnp.int32, shape, dim)


def pad_row(row, lanes):
    return jnp.concatenate([row, jnp.zeros((1, lanes - row.shape[1]), row.dtype)], axis=1)


def column(row, rows):
    shape = (rows, row.shape[1])
    picked = jnp.where(iota(shape, 0) == iota(shape, 1), jnp.broadcast_to(row, shape), 0.0)
    return jnp.sum(picked, axis=1, keepdims=True)


def kernel(
    nb, nl, total, scale,
    control, mask_in, profile_in, plume_in, courant, upwind, speed_in, factor_in, background, rate_in, weight_in, prec_in,
    obs_out, hess_out,
    bg, ctl, mask, profile, plume, cour, upw, speed, factor, rate, weight, prec,
    lhs, amp, rb, gb, bfield, face, nface, coef, ncoef, here, nhere, quot, nquot, masked, edge, kern,
    krow, mine_in, left_in, right_in, part_in, t_lev, t_left, t_right, t_own, s_own, out_buf,
    load_sem, bg_sem,
    halo_send, halo_recv, down_send, down_recv, edge_send, edge_recv,
    mine_send, mine_recv, left_send, left_recv, right_send, right_recv,
    part_send, part_recv, tl_send, tl_recv, tx_send, tx_recv, ag_send, ag_recv, near_sem, far_sem, entry_sem,
):
    lev, tile = lax.axis_index("lev"), lax.axis_index("tile")
    tiles = lax.axis_size("tile")
    before, after = lax.rem(tile + tiles - 1, tiles), lax.rem(tile + 1, tiles)
    ny = bg.shape[2]
    chunk = nb // 4
    run = min(8, tiles)
    place = lax.rem(tile, run)
    is_first, is_last = place == 0, place == run - 1
    lev_after = lev ^ jnp.where(is_last, 2, 0)
    lev_before = lev ^ jnp.where(is_first, 2, 0)
    core = lax.rem(lev, 2)
    own = pl.ds(pl.multiple_of(lev * nl, 8), nl)

    def at(lev_to, tile_to):
        return {"lev": lev_to, "tile": tile_to}

    def send(src, dst, send_sem, recv_sem, lev_to, tile_to):
        return pltpu.make_async_remote_copy(
            src_ref=src, dst_ref=dst, send_sem=send_sem, recv_sem=recv_sem,
            device_id=at(lev_to, tile_to), device_id_type=MESH,
        )

    def arrived(dst, sem):
        pltpu.make_async_copy(dst, dst, sem).wait()

    barrier = pltpu.get_barrier_semaphore()

    @pl.when(is_last)
    def _():
        pl.semaphore_wait(barrier, 4)
        for n in range(2):
            pl.semaphore_signal(near_sem, inc=1, device_id=at(lev_after - core + n, after), device_id_type=MESH)
        for n in range(2):
            pl.semaphore_signal(far_sem, inc=1, device_id=at(lev - core + n, after), device_id_type=MESH)

    for k in range(4):
        pl.semaphore_signal(barrier, inc=1, device_id=at(k, before), device_id_type=MESH)

    @pl.when(place < run - 2)
    def _():
        for k in range(4):
            pl.semaphore_signal(barrier, inc=1, device_id=at(k, after), device_id_type=MESH)

    @pl.when(jnp.logical_not(is_last))
    def _():
        for k in range(1, 4):
            pl.semaphore_signal(barrier, inc=1, device_id=at(lev ^ k, tile), device_id_type=MESH)

    small = [
        (courant.at[:, :, 0, :], cour), (upwind.at[:, :, 0, :], upw), (plume_in, plume), (control.at[:, 0, :], ctl),
        (mask_in, mask), (speed_in, speed), (factor_in, factor), (weight_in, weight), (profile_in, profile),
        (rate_in.at[:, 0, :], rate), (prec_in, prec),
    ]
    loads = [pltpu.make_async_copy(a, b, load_sem.at[n]) for n, (a, b) in enumerate(small)]
    for copy in loads:
        copy.start()

    def bg_copy(l):
        return pltpu.make_async_copy(background.at[:, l, 0, :], bg.at[l], bg_sem.at[l])

    def bg_start(l, _):
        bg_copy(l).start()
        return 0

    lax.fori_loop(0, nl, bg_start, 0)

    @pl.when(is_first)
    def _():
        pl.semaphore_wait(barrier, 7)

    @pl.when(jnp.logical_not(jnp.logical_or(is_first, is_last)))
    def _():
        pl.semaphore_wait(barrier, 11)

    @pl.when(place == run - 2)
    def _():
        for k in range(4):
            pl.semaphore_signal(entry_sem, inc=1, device_id=at(k, after), device_id_type=MESH)

    for n in range(3):
        loads[n].wait()
    plume_col = column(plume[...], nl)
    scaled = jnp.where(upw[...] == 1, cour[...], -cour[...]) * plume_col[None]
    face[0, own, :] = scaled[0]
    face[1, own, :] = scaled[1]
    face[2, own, :] = jnp.broadcast_to(plume_col, (nl, ny))
    for m in range(3):
        @pl.when(m < lev)
        def _():
            nface[m * nl:(m + 1) * nl, :] = jnp.zeros((nl, ny), F32)
    for n in range(3, 5):
        loads[n].wait()
    masked[0] = ctl[...] * mask[...].astype(F32)

    def upward(d):
        return pl.ds(d * nl, total - d * nl)

    def halo(d):
        return send(face.at[0, upward(d)], nface.at[upward(d)], halo_send.at[0], halo_recv.at[0], lev_before, before)

    def spread(k):
        return send(face.at[:, own], face.at[:, own], down_send.at[k], down_recv.at[lev], lev ^ k, tile)

    edges = [
        send(masked.at[0], edge.at[0], edge_send.at[0], edge_recv.at[0], lev_after, after),
        send(masked.at[0], edge.at[1], edge_send.at[1], edge_recv.at[1], lev_before, before),
    ]

    @pl.when(is_last)
    def _():
        edges[0].start()
        pl.semaphore_wait(entry_sem, 4)

    for k in range(1, 4):
        spread(k).start()

    @pl.when(jnp.logical_not(is_last))
    def _():
        edges[0].start()

    @pl.when(jnp.logical_not(is_first))
    def _():
        edges[1].start()

    for n in range(5, 11):
        loads[n].wait()
    row_i, lane_i = iota((nb, 128), 0), iota((nb, 128), 1)
    weight_row = pad_row(weight[...], 128)
    weight_col = column(weight_row, nb)
    shifted = jnp.broadcast_to(weight_row, (nb, 128))
    for bit in range(7):
        shifted = jnp.where((row_i >> bit) & 1 == 1, pltpu.roll(shifted, 128 - (1 << bit), 1), shifted)
    mixing = jnp.where(row_i + lane_i < nb, shifted, 0.0) - weight_row - weight_col
    mix_hi, mix_lo = split(jnp.where(lane_i < nb, mixing, 0.0))
    lhs[0:nb, 0:128] = mix_hi
    lhs[0:nb, 128:256] = mix_hi
    lhs[nb:2 * nb, 0:128] = mix_lo
    lhs[nb:2 * nb, 128:256] = jnp.zeros((nb, 128), BF16)

    speed_col = column(pad_row(speed[...], 128), nb)
    profile_col = column(pad_row(profile[...], 128), nb)
    factor_row = pad_row(factor[...], 128)
    fall = speed_col * factor_row
    above = fall / (1.0 + fall)
    fall = speed_col * pltpu.roll(jnp.broadcast_to(factor_row, (8, 128)), lax.rem(128 - lev * nl, 128), 1)[0:1]
    inverse = 1.0 / (1.0 + fall)
    gain = fall * inverse
    for l in range(nl):
        rb[l] = jnp.broadcast_to(inverse[:, l:l + 1], (nb, 128))
        gb[l] = jnp.broadcast_to(gain[:, l:l + 1], (nb, 128))
    chain = jnp.where(lane_i < (lev + 1) * nl, 1.0, above)
    step = 1
    while step < total:
        chain = chain * jnp.where(lane_i >= step, pltpu.roll(chain, step, 1), 1.0)
        step *= 2
    chain = jnp.where(lane_i < (lev + 1) * nl, 0.0, chain)[:, 0:total]

    masked[1] = pltpu.roll(masked[0], 1, 1)
    masked[2] = pltpu.roll(masked[0], ny - 1, 1)

    def mix_level(l, _):
        bg_copy(l).wait()
        hi, lo = split(bg[l])
        rest = jnp.zeros((128 - nb, ny), BF16)
        both = jnp.dot(lhs[...], jnp.concatenate([hi, rest, lo, rest], axis=0), preferred_element_type=F32)
        amp[l] = weight_col + rate[pl.ds(l, 1), :] * (both[0:nb] + both[nb:2 * nb])
        return 0

    lax.fori_loop(0, nl, mix_level, 0)

    def rows_of(c):
        return pl.ds(pl.multiple_of(c * chunk, 8), chunk)

    def wide(value):
        return jnp.concatenate([value] * (ny // 128), axis=1)

    rb[nl] = jnp.broadcast_to(profile_col, (nb, 128))

    def settle(c, _):
        rows = rows_of(c)
        value = jnp.zeros((chunk, ny), F32)
        for l in range(nl):
            value = amp[l, rows, :] * wide(rb[l, rows, :]) + value * wide(gb[l, rows, :])
            bfield[l, rows, :] = value
        return 0

    lax.fori_loop(0, 4, settle, 0)

    def faces():
        for k in range(1, 4):
            d = lev ^ k
            arrived(face.at[:, pl.ds(pl.multiple_of(d * nl, 8), nl)], down_recv.at[d])

    def send_halos():
        for d in range(4):
            @pl.when(d == lev_before)
            def _():
                halo(d).start()

    @pl.when(jnp.logical_not(is_last))
    def _():
        faces()

    @pl.when(is_first)
    def _():
        pl.semaphore_wait(near_sem, 2)

    @pl.when(jnp.logical_not(is_last))
    def _():
        send_halos()

    @pl.when(is_first)
    def _():
        edges[1].start()
        pl.semaphore_wait(far_sem, 2)

    for d in range(4):
        @pl.when(d == lev)
        def _():
            arrived(nface.at[upward(d)], halo_recv.at[0])
    inflow = -jnp.minimum(nface[...], 0.0)
    ncoef[...] = inflow
    nhere[...] = ncoef[own, :]
    nquot[...] = dot3(chain, inflow)

    def right(c):
        part = lax.rem(c, 2)
        return send(
            krow.at[rows_of(c)], right_in.at[part, core], right_send.at[c], right_recv.at[2 * part + core],
            lev_after - core + c // 2, after,
        )

    def next_row(i, _):
        c = lax.rem(2 * i, 4) + i // 2
        rows = rows_of(c)
        total_in = jnp.zeros((chunk, ny), F32)
        for l in range(nl):
            total_in = total_in + bfield[l, rows, :] * nhere[l:l + 1, :]
        krow[rows, :] = wide(rb[nl, rows, :]) * (total_in + bfield[nl - 1, rows, :] * nquot[rows, :])
        right(c).start()
        return 0

    lax.fori_loop(0, 4, next_row, 0)

    @pl.when(is_last)
    def _():
        faces()
        send_halos()

    face_x, face_y = face[0], face[1]
    next_y = pltpu.roll(face_y, ny - 1, 1)
    coef[0] = jnp.maximum(face_y, 0.0)
    coef[1] = -jnp.minimum(next_y, 0.0)
    coef[2] = (
        face[2] + jnp.minimum(face_x, 0.0) + jnp.minimum(face_y, 0.0) - jnp.maximum(next_y, 0.0)
        - jnp.maximum(nface[...], 0.0)
    )
    coef[3] = jnp.maximum(face_x, 0.0)
    for n in range(4):
        quot[n] = dot3(chain, coef[n])
        here[n] = coef[n, own, :]

    def mine_to(c):
        return send(kern.at[c, pl.ds(0, 3)], mine_in.at[lev], mine_send.at[c], mine_recv.at[lev], c, tile)

    def left(c):
        return send(kern.at[c, 3], left_in.at[lev], left_send.at[c], left_recv.at[lev], c, before)

    def others(c, t_sum):
        rows = rows_of(c)
        sums = [jnp.zeros((chunk, ny), F32) for _ in range(4)]
        for l in range(nl):
            value = bfield[l, rows, :]
            for n in range(4):
                sums[n] = sums[n] + value * here[n, l:l + 1, :]
        prof = wide(rb[nl, rows, :])
        value = bfield[nl - 1, rows, :]
        sums = [prof * (sums[n] + value * quot[n, rows, :]) for n in range(4)]
        for n in range(4):
            kern[c, n] = sums[n]

        @pl.when(c != lev)
        def _():
            mine_to(c).start()
        left(c).start()
        part = masked[0, rows, :] * sums[2] + masked[1, rows, :] * sums[0] + masked[2, rows, :] * sums[1]
        for r in range(0, chunk, 8):
            t_sum = t_sum + part[r:r + 8]
        return t_sum

    t_sum = lax.fori_loop(0, 4, others, jnp.zeros((8, ny), F32))
    for n in range(2):
        arrived(edge.at[n], edge_recv.at[n])
    for c in range(4):
        rows = pl.ds(c * chunk, chunk)
        part = edge[0, rows, :] * kern[c, 3] + edge[1, rows, :] * krow[rows, :]
        for r in range(0, chunk, 8):
            t_sum = t_sum + part[r:r + 8]
    t_mine = jnp.sum(t_sum, axis=0, keepdims=True) * scale
    s_mine = t_mine * prec[...] * scale
    t_own[...] = t_mine
    s_own[...] = s_mine

    t_sends = []
    for k in range(4):
        t_sends.append(send(s_own, t_left.at[lev], tx_send.at[k], tx_recv.at[lev], k, after))
        t_sends.append(send(s_own, t_right.at[lev], tx_send.at[4 + k], tx_recv.at[4 + lev], k, before))
    for k in range(1, 4):
        t_sends.append(send(t_own, t_lev.at[k], tl_send.at[k], tl_recv.at[k], lev ^ k, tile))
    for copy in t_sends:
        copy.start()

    def part(n, k):
        return send(
            part_in.at[lev, n], part_in.at[lev, n], part_send.at[4 * n + k], part_recv.at[4 * n + lev], lev ^ k, tile
        )

    def from_before():
        for n in range(2):
            for k in range(2):
                arrived(right_in.at[n, k], right_recv.at[2 * n + k])
            part_in[lev, n] = right_in[n, 0] + right_in[n, 1]
            for k in range(1, 4):
                part(n, k).start()

    @pl.when(jnp.logical_not(is_first))
    def _():
        from_before()

    totals = [kern[lev, n] for n in range(3)]
    for k in range(1, 4):
        d = lev ^ k
        arrived(mine_in.at[d], mine_recv.at[d])
        totals = [totals[n] + mine_in[d, n] for n in range(3)]
    t_all = t_mine
    for k in range(1, 4):
        arrived(t_lev.at[k], tl_recv.at[k])
        t_all = t_all + t_lev[k]
    obs_out[...] = t_all
    s_here = t_all * prec[...] * scale
    result = totals[2] * s_here + pltpu.roll(totals[0] * s_here, ny - 1, 1) + pltpu.roll(totals[1] * s_here, 1, 1)
    for k in range(4):
        arrived(left_in.at[k], left_recv.at[k])
    from_after = (left_in[0] + left_in[1]) + (left_in[2] + left_in[3])
    for k in range(4):
        arrived(t_right.at[k], tx_recv.at[4 + k])
    s_after = (t_right[0] + t_right[1]) + (t_right[2] + t_right[3])
    mine = rows_of(lev)
    out_buf[mine, :] = result + from_after * s_after
    gathers = [
        send(out_buf.at[mine], out_buf.at[mine], ag_send.at[k], ag_recv.at[lev], lev ^ k, tile) for k in range(1, 4)
    ]
    for copy in gathers:
        copy.start()

    @pl.when(is_first)
    def _():
        from_before()

    for d in range(4):
        @pl.when(d == lev_before)
        def _():
            halo(d).wait_send()
    for k in range(1, 4):
        spread(k).wait_send()
    for copy in edges + t_sends:
        copy.wait_send()
    for c in range(4):
        @pl.when(c != lev)
        def _():
            mine_to(c).wait_send()
        left(c).wait_send()
        right(c).wait_send()

    for copy in gathers:
        copy.wait_send()

    for k in range(4):
        arrived(t_left.at[k], tx_recv.at[k])
    s_before = (t_left[0] + t_left[1]) + (t_left[2] + t_left[3])
    for k in range(1, 4):
        d = lev ^ k
        arrived(out_buf.at[rows_of(d)], ag_recv.at[d])
    mask_row = mask[...].astype(F32)
    for n in range(2):
        for k in range(1, 4):
            d = lev ^ k
            arrived(part_in.at[d, n], part_recv.at[4 * n + d])
        for h in range(2):
            rows = pl.ds((2 * h + n) * chunk, chunk)
            hess_out[rows, :] = mask_row * (out_buf[rows, :] + (part_in[h, n] + part_in[2 + h, n]) * s_before)
    for n in range(2):
        for k in range(1, 4):
            part(n, k).wait_send()


def per_device(
    control, emit_mask, bin_profile, plume_profile, courant, upwind, bin_speed, level_factor, background, coag_rate,
    obs_weight, obs_precision,
):
    nb, nl, _, ny = background.shape
    total = level_factor.shape[0]
    chunk = nb // 4
    vmem, dma = pltpu.VMEM, pltpu.SemaphoreType.DMA
    obs, hess = pl.pallas_call(
        functools.partial(kernel, nb, nl, total, 1.0 / (nb * total)),
        out_shape=(jax.ShapeDtypeStruct((1, ny), F32), jax.ShapeDtypeStruct((nb, ny), F32)),
        in_specs=[pl.BlockSpec(memory_space=pl.ANY)] * 12,
        out_specs=(pl.BlockSpec(memory_space=pltpu.VMEM),) * 2,
        scratch_shapes=[
            vmem((nl, nb, ny), F32),
            vmem((nb, ny), F32),
            vmem((1, ny), jnp.int32),
            vmem((1, nb), F32),
            vmem((1, nl), F32),
            vmem((2, nl, ny), F32),
            vmem((2, nl, ny), jnp.int32),
            vmem((1, nb), F32),
            vmem((1, total), F32),
            vmem((nl, ny), F32),
            vmem((1, nb), F32),
            vmem((1, ny), F32),
            vmem((2 * nb, 256), BF16),
            vmem((nl, nb, ny), F32),
            vmem((nl + 1, nb, 128), F32),
            vmem((nl, nb, 128), F32),
            vmem((nl, nb, ny), F32),
            vmem((3, total, ny), F32),
            vmem((total, ny), F32),
            vmem((4, total, ny), F32),
            vmem((total, ny), F32),
            vmem((4, nl, ny), F32),
            vmem((nl, ny), F32),
            vmem((4, nb, ny), F32),
            vmem((nb, ny), F32),
            vmem((3, nb, ny), F32),
            vmem((2, nb, ny), F32),
            vmem((4, 4, chunk, ny), F32),
            vmem((nb, ny), F32),
            vmem((4, 3, chunk, ny), F32),
            vmem((4, chunk, ny), F32),
            vmem((2, 2, chunk, ny), F32),
            vmem((4, 2, chunk, ny), F32),
            vmem((4, 1, ny), F32),
            vmem((4, 1, ny), F32),
            vmem((4, 1, ny), F32),
            vmem((1, ny), F32),
            vmem((1, ny), F32),
            vmem((nb, ny), F32),
            dma((11,)), dma((nl,)),
            dma((4,)), dma((4,)), dma((4,)), dma((4,)), dma((2,)), dma((2,)),
            dma((4,)), dma((4,)), dma((4,)), dma((4,)), dma((4,)), dma((4,)),
            dma((8,)), dma((8,)), dma((4,)), dma((4,)), dma((8,)), dma((8,)), dma((4,)), dma((4,)),
            pltpu.SemaphoreType.REGULAR, pltpu.SemaphoreType.REGULAR, pltpu.SemaphoreType.REGULAR,
        ],
        compiler_params=pltpu.CompilerParams(collective_id=0, has_side_effects=True, vmem_limit_bytes=24 << 20),
        name="hessian",
    )(*[
        pltpu.with_memory_space_constraint(value, pltpu.HBM) for value in (
            control, emit_mask, bin_profile[None], plume_profile[None], courant, upwind, bin_speed[None],
            level_factor[None], background, coag_rate, obs_weight[None], obs_precision,
        )
    ])
    return obs, hess[:, None, :]


def solution(mesh):
    in_specs = (
        P(None, "tile", None), P("tile", None), P(), P("lev"), P(None, "lev", "tile", None), P(None, "lev", "tile", None),
        P(), P(), P(None, "lev", "tile", None), P("lev", "tile", None), P(), P("tile", None),
    )
    out_specs = (P("tile", None), P(None, "tile", None))
    return jax.shard_map(per_device, mesh=mesh, in_specs=in_specs, out_specs=out_specs, check_vma=False)
```

```python
import functools

import jax
import jax.numpy as jnp
from jax import lax
from jax.experimental import pallas as pl
from jax.experimental.pallas import tpu as pltpu
from jax.sharding import PartitionSpec as P

MESH = pl.DeviceIdType.MESH
F32, BF16 = jnp.float32, jnp.bfloat16


def split(value):
    high = value.astype(BF16)
    return high, (value - high.astype(F32)).astype(BF16)


def dot3(a, b):
    a_hi, a_lo = split(a)
    b_hi, b_lo = split(b)
    dot = functools.partial(jnp.dot, preferred_element_type=F32)
    return dot(a_hi, b_hi) + (dot(a_hi, b_lo) + dot(a_lo, b_hi))


def iota(shape, dim):
    return lax.broadcasted_iota(jnp.int32, shape, dim)


def pad_row(row, lanes):
    return jnp.concatenate([row, jnp.zeros((1, lanes - row.shape[1]), row.dtype)], axis=1)


def column(row, rows):
    shape = (rows, row.shape[1])
    picked = jnp.where(iota(shape, 0) == iota(shape, 1), jnp.broadcast_to(row, shape), 0.0)
    return jnp.sum(picked, axis=1, keepdims=True)


def kernel(
    nb, nl, total, scale,
    control, mask_in, profile_in, plume_in, courant, upwind, speed_in, factor_in, background, rate_in, weight_in, prec_in,
    obs_out, hess_out,
    bg, ctl, mask, profile, plume, cour, upw, speed, factor, rate, weight, prec,
    lhs, amp, rb, gb, bfield, face, nface, coef, ncoef, here, nhere, quot, nquot, masked, edge, kern,
    krow, mine_in, left_in, right_in, part_in, t_lev, t_left, t_right, t_own, s_own, out_buf,
    load_sem, bg_sem,
    halo_send, halo_recv, down_send, down_recv, edge_send, edge_recv,
    mine_send, mine_recv, left_send, left_recv, right_send, right_recv,
    part_send, part_recv, tl_send, tl_recv, tx_send, tx_recv, ag_send, ag_recv, near_sem, far_sem, entry_sem,
):
    lev, tile = lax.axis_index("lev"), lax.axis_index("tile")
    tiles = lax.axis_size("tile")
    before, after = lax.rem(tile + tiles - 1, tiles), lax.rem(tile + 1, tiles)
    ny = bg.shape[2]
    chunk = nb // 4
    run = min(8, tiles)
    place = lax.rem(tile, run)
    is_first, is_last = place == 0, place == run - 1
    lev_after = lev ^ jnp.where(is_last, 2, 0)
    lev_before = lev ^ jnp.where(is_first, 2, 0)
    core = lax.rem(lev, 2)
    own = pl.ds(pl.multiple_of(lev * nl, 8), nl)

    def at(lev_to, tile_to):
        return {"lev": lev_to, "tile": tile_to}

    def send(src, dst, send_sem, recv_sem, lev_to, tile_to):
        return pltpu.make_async_remote_copy(
            src_ref=src, dst_ref=dst, send_sem=send_sem, recv_sem=recv_sem,
            device_id=at(lev_to, tile_to), device_id_type=MESH,
        )

    def arrived(dst, sem):
        pltpu.make_async_copy(dst, dst, sem).wait()

    barrier = pltpu.get_barrier_semaphore()

    @pl.when(is_last)
    def _():
        pl.semaphore_wait(barrier, 4)
        for n in range(2):
            pl.semaphore_signal(near_sem, inc=1, device_id=at(lev_after - core + n, after), device_id_type=MESH)
        for n in range(2):
            pl.semaphore_signal(far_sem, inc=1, device_id=at(lev - core + n, after), device_id_type=MESH)

    for k in range(4):
        pl.semaphore_signal(barrier, inc=1, device_id=at(k, before), device_id_type=MESH)

    @pl.when(place < run - 2)
    def _():
        for k in range(4):
            pl.semaphore_signal(barrier, inc=1, device_id=at(k, after), device_id_type=MESH)

    @pl.when(jnp.logical_not(is_last))
    def _():
        for k in range(1, 4):
            pl.semaphore_signal(barrier, inc=1, device_id=at(lev ^ k, tile), device_id_type=MESH)

    small = [
        (courant.at[:, :, 0, :], cour), (upwind.at[:, :, 0, :], upw), (plume_in, plume), (control.at[:, 0, :], ctl),
        (mask_in, mask), (speed_in, speed), (factor_in, factor), (weight_in, weight), (profile_in, profile),
        (rate_in.at[:, 0, :], rate), (prec_in, prec),
    ]
    loads = [pltpu.make_async_copy(a, b, load_sem.at[n]) for n, (a, b) in enumerate(small)]
    for copy in loads:
        copy.start()

    def bg_copy(l):
        return pltpu.make_async_copy(background.at[:, l, 0, :], bg.at[l], bg_sem.at[l])

    def bg_start(l, _):
        bg_copy(l).start()
        return 0

    lax.fori_loop(0, nl, bg_start, 0)

    @pl.when(is_first)
    def _():
        pl.semaphore_wait(barrier, 7)

    @pl.when(jnp.logical_not(jnp.logical_or(is_first, is_last)))
    def _():
        pl.semaphore_wait(barrier, 11)

    @pl.when(place == run - 2)
    def _():
        for k in range(4):
            pl.semaphore_signal(entry_sem, inc=1, device_id=at(k, after), device_id_type=MESH)

    for n in range(3):
        loads[n].wait()
    plume_col = column(plume[...], nl)
    scaled = jnp.where(upw[...] == 1, cour[...], -cour[...]) * plume_col[None]
    face[0, own, :] = scaled[0]
    face[1, own, :] = scaled[1]
    face[2, own, :] = jnp.broadcast_to(plume_col, (nl, ny))
    for m in range(3):
        @pl.when(m < lev)
        def _():
            nface[m * nl:(m + 1) * nl, :] = jnp.zeros((nl, ny), F32)
    for n in range(3, 5):
        loads[n].wait()
    masked[0] = ctl[...] * mask[...].astype(F32)

    def upward(d):
        return pl.ds(d * nl, total - d * nl)

    def halo(d):
        return send(face.at[0, upward(d)], nface.at[upward(d)], halo_send.at[0], halo_recv.at[0], lev_before, before)

    def spread(k):
        return send(face.at[:, own], face.at[:, own], down_send.at[k], down_recv.at[lev], lev ^ k, tile)

    edges = [
        send(masked.at[0], edge.at[0], edge_send.at[0], edge_recv.at[0], lev_after, after),
        send(masked.at[0], edge.at[1], edge_send.at[1], edge_recv.at[1], lev_before, before),
    ]

    @pl.when(is_last)
    def _():
        edges[0].start()
        pl.semaphore_wait(entry_sem, 4)

    for k in range(1, 4):
        spread(k).start()

    @pl.when(jnp.logical_not(is_last))
    def _():
        edges[0].start()

    @pl.when(jnp.logical_not(is_first))
    def _():
        edges[1].start()

    for n in range(5, 11):
        loads[n].wait()
    row_i, lane_i = iota((nb, 128), 0), iota((nb, 128), 1)
    weight_row = pad_row(weight[...], 128)
    weight_col = column(weight_row, nb)
    shifted = jnp.broadcast_to(weight_row, (nb, 128))
    for bit in range(7):
        shifted = jnp.where((row_i >> bit) & 1 == 1, pltpu.roll(shifted, 128 - (1 << bit), 1), shifted)
    mixing = jnp.where(row_i + lane_i < nb, shifted, 0.0) - weight_row - weight_col
    mix_hi, mix_lo = split(jnp.where(lane_i < nb, mixing, 0.0))
    lhs[0:nb, 0:128] = mix_hi
    lhs[0:nb, 128:256] = mix_hi
    lhs[nb:2 * nb, 0:128] = mix_lo
    lhs[nb:2 * nb, 128:256] = jnp.zeros((nb, 128), BF16)

    speed_col = column(pad_row(speed[...], 128), nb)
    profile_col = column(pad_row(profile[...], 128), nb)
    factor_row = pad_row(factor[...], 128)
    fall = speed_col * factor_row
    above = fall / (1.0 + fall)
    fall = speed_col * pltpu.roll(jnp.broadcast_to(factor_row, (8, 128)), lax.rem(128 - lev * nl, 128), 1)[0:1]
    inverse = 1.0 / (1.0 + fall)
    gain = fall * inverse
    for l in range(nl):
        rb[l] = jnp.broadcast_to(inverse[:, l:l + 1], (nb, 128))
        gb[l] = jnp.broadcast_to(gain[:, l:l + 1], (nb, 128))
    chain = jnp.where(lane_i < (lev + 1) * nl, 1.0, above)
    step = 1
    while step < total:
        chain = chain * jnp.where(lane_i >= step, pltpu.roll(chain, step, 1), 1.0)
        step *= 2
    chain = jnp.where(lane_i < (lev + 1) * nl, 0.0, chain)[:, 0:total]

    masked[1] = pltpu.roll(masked[0], 1, 1)
    masked[2] = pltpu.roll(masked[0], ny - 1, 1)

    def mix_level(l, _):
        bg_copy(l).wait()
        hi, lo = split(bg[l])
        rest = jnp.zeros((128 - nb, ny), BF16)
        both = jnp.dot(lhs[...], jnp.concatenate([hi, rest, lo, rest], axis=0), preferred_element_type=F32)
        amp[l] = weight_col + rate[pl.ds(l, 1), :] * (both[0:nb] + both[nb:2 * nb])
        return 0

    lax.fori_loop(0, nl, mix_level, 0)

    def rows_of(c):
        return pl.ds(pl.multiple_of(c * chunk, 8), chunk)

    def wide(value):
        return jnp.concatenate([value] * (ny // 128), axis=1)

    rb[nl] = jnp.broadcast_to(profile_col, (nb, 128))

    def settle(c, _):
        rows = rows_of(c)
        value = jnp.zeros((chunk, ny), F32)
        for l in range(nl):
            value = amp[l, rows, :] * wide(rb[l, rows, :]) + value * wide(gb[l, rows, :])
            bfield[l, rows, :] = value
        return 0

    lax.fori_loop(0, 4, settle, 0)

    def faces():
        for k in range(1, 4):
            d = lev ^ k
            arrived(face.at[:, pl.ds(pl.multiple_of(d * nl, 8), nl)], down_recv.at[d])

    def send_halos():
        for d in range(4):
            @pl.when(d == lev_before)
            def _():
                halo(d).start()

    @pl.when(jnp.logical_not(is_last))
    def _():
        faces()

    @pl.when(is_first)
    def _():
        pl.semaphore_wait(near_sem, 2)

    @pl.when(jnp.logical_not(is_last))
    def _():
        send_halos()

    @pl.when(is_first)
    def _():
        edges[1].start()
        pl.semaphore_wait(far_sem, 2)

    for d in range(4):
        @pl.when(d == lev)
        def _():
            arrived(nface.at[upward(d)], halo_recv.at[0])
    inflow = -jnp.minimum(nface[...], 0.0)
    ncoef[...] = inflow
    nhere[...] = ncoef[own, :]
    nquot[...] = dot3(chain, inflow)

    def right(c):
        return send(
            krow.at[rows_of(c)], right_in.at[0, core], right_send.at[c], right_recv.at[core], lev_after - core + c // 2, after
        )

    def right_both(c, to):
        return send(
            krow.at[rows_of(c)], right_in.at[1, lev], right_send.at[4 + 2 * (c // 2) + to // 2], right_recv.at[4 + lev],
            to + c // 2, after,
        )

    def next_row(i, _):
        c = lax.rem(2 * i, 4) + i // 2
        rows = rows_of(c)
        total_in = jnp.zeros((chunk, ny), F32)
        for l in range(nl):
            total_in = total_in + bfield[l, rows, :] * nhere[l:l + 1, :]
        krow[rows, :] = wide(rb[nl, rows, :]) * (total_in + bfield[nl - 1, rows, :] * nquot[rows, :])
        @pl.when(i < 2)
        def _():
            right(c).start()

        @pl.when(i >= 2)
        def _():
            for to in (0, 2):
                right_both(c, to).start()
        return 0

    lax.fori_loop(0, 4, next_row, 0)

    @pl.when(is_last)
    def _():
        faces()
        send_halos()

    face_x, face_y = face[0], face[1]
    next_y = pltpu.roll(face_y, ny - 1, 1)
    coef[0] = jnp.maximum(face_y, 0.0)
    coef[1] = -jnp.minimum(next_y, 0.0)
    coef[2] = (
        face[2] + jnp.minimum(face_x, 0.0) + jnp.minimum(face_y, 0.0) - jnp.maximum(next_y, 0.0)
        - jnp.maximum(nface[...], 0.0)
    )
    coef[3] = jnp.maximum(face_x, 0.0)
    for n in range(4):
        quot[n] = dot3(chain, coef[n])
        here[n] = coef[n, own, :]

    def mine_to(c):
        return send(kern.at[c, pl.ds(0, 3)], mine_in.at[lev], mine_send.at[c], mine_recv.at[lev], c, tile)

    def left(c):
        return send(kern.at[c, 3], left_in.at[lev], left_send.at[c], left_recv.at[lev], c, before)

    def others(c, t_sum):
        rows = rows_of(c)
        sums = [jnp.zeros((chunk, ny), F32) for _ in range(4)]
        for l in range(nl):
            value = bfield[l, rows, :]
            for n in range(4):
                sums[n] = sums[n] + value * here[n, l:l + 1, :]
        prof = wide(rb[nl, rows, :])
        value = bfield[nl - 1, rows, :]
        sums = [prof * (sums[n] + value * quot[n, rows, :]) for n in range(4)]
        for n in range(4):
            kern[c, n] = sums[n]

        @pl.when(c != lev)
        def _():
            mine_to(c).start()
        left(c).start()
        part = masked[0, rows, :] * sums[2] + masked[1, rows, :] * sums[0] + masked[2, rows, :] * sums[1]
        for r in range(0, chunk, 8):
            t_sum = t_sum + part[r:r + 8]
        return t_sum

    t_sum = lax.fori_loop(0, 4, others, jnp.zeros((8, ny), F32))
    for n in range(2):
        arrived(edge.at[n], edge_recv.at[n])
    for c in range(4):
        rows = pl.ds(c * chunk, chunk)
        part = edge[0, rows, :] * kern[c, 3] + edge[1, rows, :] * krow[rows, :]
        for r in range(0, chunk, 8):
            t_sum = t_sum + part[r:r + 8]
    t_mine = jnp.sum(t_sum, axis=0, keepdims=True) * scale
    s_mine = t_mine * prec[...] * scale
    t_own[...] = t_mine
    s_own[...] = s_mine

    t_sends = []
    for k in range(4):
        t_sends.append(send(s_own, t_left.at[lev], tx_send.at[k], tx_recv.at[lev], k, after))
        t_sends.append(send(s_own, t_right.at[lev], tx_send.at[4 + k], tx_recv.at[4 + lev], k, before))
    for k in range(1, 4):
        t_sends.append(send(t_own, t_lev.at[k], tl_send.at[k], tl_recv.at[k], lev ^ k, tile))
    for copy in t_sends:
        copy.start()

    def part(n, k):
        return send(
            part_in.at[lev, n], part_in.at[lev, n], part_send.at[4 * n + k], part_recv.at[4 * n + lev], lev ^ k, tile
        )

    def from_before():
        for k in range(2):
            arrived(right_in.at[0, k], right_recv.at[k])
        part_in[lev, 0] = right_in[0, 0] + right_in[0, 1]
        for k in range(1, 4):
            part(0, k).start()
        for k in range(4):
            arrived(right_in.at[1, k], right_recv.at[4 + k])
        part_in[lev, 1] = (right_in[1, 0] + right_in[1, 1]) + (right_in[1, 2] + right_in[1, 3])
        part(1, 1).start()

    @pl.when(jnp.logical_not(is_first))
    def _():
        from_before()

    totals = [kern[lev, n] for n in range(3)]
    for k in range(1, 4):
        d = lev ^ k
        arrived(mine_in.at[d], mine_recv.at[d])
        totals = [totals[n] + mine_in[d, n] for n in range(3)]
    t_all = t_mine
    for k in range(1, 4):
        arrived(t_lev.at[k], tl_recv.at[k])
        t_all = t_all + t_lev[k]
    obs_out[...] = t_all
    s_here = t_all * prec[...] * scale
    result = totals[2] * s_here + pltpu.roll(totals[0] * s_here, ny - 1, 1) + pltpu.roll(totals[1] * s_here, 1, 1)
    for k in range(4):
        arrived(left_in.at[k], left_recv.at[k])
    from_after = (left_in[0] + left_in[1]) + (left_in[2] + left_in[3])
    for k in range(4):
        arrived(t_right.at[k], tx_recv.at[4 + k])
    s_after = (t_right[0] + t_right[1]) + (t_right[2] + t_right[3])
    mine = rows_of(lev)
    out_buf[mine, :] = result + from_after * s_after
    gathers = [
        send(out_buf.at[mine], out_buf.at[mine], ag_send.at[k], ag_recv.at[lev], lev ^ k, tile) for k in range(1, 4)
    ]
    for copy in gathers:
        copy.start()

    @pl.when(is_first)
    def _():
        from_before()

    for d in range(4):
        @pl.when(d == lev_before)
        def _():
            halo(d).wait_send()
    for k in range(1, 4):
        spread(k).wait_send()
    for h in range(2):
        right(2 * h).wait_send()
        for to in (0, 2):
            right_both(2 * h + 1, to).wait_send()
    for copy in edges + t_sends:
        copy.wait_send()
    for c in range(4):
        @pl.when(c != lev)
        def _():
            mine_to(c).wait_send()
        left(c).wait_send()

    for copy in gathers:
        copy.wait_send()

    for k in range(4):
        arrived(t_left.at[k], tx_recv.at[k])
    s_before = (t_left[0] + t_left[1]) + (t_left[2] + t_left[3])
    for k in range(1, 4):
        d = lev ^ k
        arrived(out_buf.at[rows_of(d)], ag_recv.at[d])
    mask_row = mask[...].astype(F32)
    arrived(part_in.at[lev ^ 1, 1], part_recv.at[4 + (lev ^ 1)])
    for h in range(2):
        rows = pl.ds((2 * h + 1) * chunk, chunk)
        hess_out[rows, 0, :] = mask_row * (out_buf[rows, :] + part_in[lev - core + h, 1] * s_before)
    for k in range(1, 4):
        d = lev ^ k
        arrived(part_in.at[d, 0], part_recv.at[d])
    for h in range(2):
        rows = pl.ds(2 * h * chunk, chunk)
        hess_out[rows, 0, :] = mask_row * (out_buf[rows, :] + (part_in[h, 0] + part_in[2 + h, 0]) * s_before)
    for k in range(1, 4):
        part(0, k).wait_send()
    part(1, 1).wait_send()


def per_device(
    control, emit_mask, bin_profile, plume_profile, courant, upwind, bin_speed, level_factor, background, coag_rate,
    obs_weight, obs_precision,
):
    nb, nl, _, ny = background.shape
    total = level_factor.shape[0]
    chunk = nb // 4
    vmem, dma = pltpu.VMEM, pltpu.SemaphoreType.DMA
    obs, hess = pl.pallas_call(
        functools.partial(kernel, nb, nl, total, 1.0 / (nb * total)),
        out_shape=(jax.ShapeDtypeStruct((1, ny), F32), jax.ShapeDtypeStruct((nb, 1, ny), F32)),
        in_specs=[pl.BlockSpec(memory_space=pl.ANY)] * 12,
        out_specs=(pl.BlockSpec(memory_space=pltpu.VMEM),) * 2,
        scratch_shapes=[
            vmem((nl, nb, ny), F32),
            vmem((nb, ny), F32),
            vmem((1, ny), jnp.int32),
            vmem((1, nb), F32),
            vmem((1, nl), F32),
            vmem((2, nl, ny), F32),
            vmem((2, nl, ny), jnp.int32),
            vmem((1, nb), F32),
            vmem((1, total), F32),
            vmem((nl, ny), F32),
            vmem((1, nb), F32),
            vmem((1, ny), F32),
            vmem((2 * nb, 256), BF16),
            vmem((nl, nb, ny), F32),
            vmem((nl + 1, nb, 128), F32),
            vmem((nl, nb, 128), F32),
            vmem((nl, nb, ny), F32),
            vmem((3, total, ny), F32),
            vmem((total, ny), F32),
            vmem((4, total, ny), F32),
            vmem((total, ny), F32),
            vmem((4, nl, ny), F32),
            vmem((nl, ny), F32),
            vmem((4, nb, ny), F32),
            vmem((nb, ny), F32),
            vmem((3, nb, ny), F32),
            vmem((2, nb, ny), F32),
            vmem((4, 4, chunk, ny), F32),
            vmem((nb, ny), F32),
            vmem((4, 3, chunk, ny), F32),
            vmem((4, chunk, ny), F32),
            vmem((2, 4, chunk, ny), F32),
            vmem((4, 2, chunk, ny), F32),
            vmem((4, 1, ny), F32),
            vmem((4, 1, ny), F32),
            vmem((4, 1, ny), F32),
            vmem((1, ny), F32),
            vmem((1, ny), F32),
            vmem((nb, ny), F32),
            dma((11,)), dma((nl,)),
            dma((4,)), dma((4,)), dma((4,)), dma((4,)), dma((2,)), dma((2,)),
            dma((4,)), dma((4,)), dma((4,)), dma((4,)), dma((8,)), dma((8,)),
            dma((8,)), dma((8,)), dma((4,)), dma((4,)), dma((8,)), dma((8,)), dma((4,)), dma((4,)),
            pltpu.SemaphoreType.REGULAR, pltpu.SemaphoreType.REGULAR, pltpu.SemaphoreType.REGULAR,
        ],
        compiler_params=pltpu.CompilerParams(collective_id=0, has_side_effects=True, vmem_limit_bytes=24 << 20),
        name="hessian",
    )(*[
        pltpu.with_memory_space_constraint(value, pltpu.HBM) for value in (
            control, emit_mask, bin_profile[None], plume_profile[None], courant, upwind, bin_speed[None],
            level_factor[None], background, coag_rate, obs_weight[None], obs_precision,
        )
    ])
    return obs, hess


def solution(mesh):
    in_specs = (
        P(None, "tile", None), P("tile", None), P(), P("lev"), P(None, "lev", "tile", None), P(None, "lev", "tile", None),
        P(), P(), P(None, "lev", "tile", None), P("lev", "tile", None), P(), P("tile", None),
    )
    out_specs = (P("tile", None), P(None, "tile", None))
    return jax.shard_map(per_device, mesh=mesh, in_specs=in_specs, out_specs=out_specs, check_vma=False)
```

```python
import functools

import jax
import jax.numpy as jnp
from jax import lax
from jax.experimental import pallas as pl
from jax.experimental.pallas import tpu as pltpu
from jax.sharding import PartitionSpec as P

MESH = pl.DeviceIdType.MESH
F32, BF16 = jnp.float32, jnp.bfloat16


def split(value):
    high = value.astype(BF16)
    return high, (value - high.astype(F32)).astype(BF16)


def dot3(a, b):
    a_hi, a_lo = split(a)
    b_hi, b_lo = split(b)
    dot = functools.partial(jnp.dot, preferred_element_type=F32)
    return dot(a_hi, b_hi) + (dot(a_hi, b_lo) + dot(a_lo, b_hi))


def iota(shape, dim):
    return lax.broadcasted_iota(jnp.int32, shape, dim)


def pad_row(row, lanes):
    return jnp.concatenate([row, jnp.zeros((1, lanes - row.shape[1]), row.dtype)], axis=1)


def column(row, rows):
    shape = (rows, row.shape[1])
    picked = jnp.where(iota(shape, 0) == iota(shape, 1), jnp.broadcast_to(row, shape), 0.0)
    return jnp.sum(picked, axis=1, keepdims=True)


def kernel(
    nb, nl, total, scale,
    control, mask_in, profile_in, plume_in, courant, upwind, speed_in, factor_in, background, rate_in, weight_in, prec_in,
    obs_out, hess_out,
    bg, ctl, mask, profile, plume, cour, upw, speed, factor, rate, weight, prec,
    lhs, amp, rb, gb, bfield, face, nface, coef, ncoef, here, nhere, quot, nquot, masked, edge, kern,
    krow, mine_in, left_in, right_in, part_in, t_lev, t_left, t_right, t_own, s_own, out_buf,
    load_sem, bg_sem,
    halo_send, halo_recv, down_send, down_recv, edge_send, edge_recv,
    mine_send, mine_recv, left_send, left_recv, right_send, right_recv,
    part_send, part_recv, tl_send, tl_recv, tx_send, tx_recv, ag_send, ag_recv, near_sem, far_sem, entry_sem,
):
    lev, tile = lax.axis_index("lev"), lax.axis_index("tile")
    tiles = lax.axis_size("tile")
    before, after = lax.rem(tile + tiles - 1, tiles), lax.rem(tile + 1, tiles)
    ny = bg.shape[2]
    chunk = nb // 4
    run = min(8, tiles)
    place = lax.rem(tile, run)
    is_first, is_last = place == 0, place == run - 1
    lev_after = lev ^ jnp.where(is_last, 2, 0)
    lev_before = lev ^ jnp.where(is_first, 2, 0)
    core = lax.rem(lev, 2)
    own = pl.ds(pl.multiple_of(lev * nl, 8), nl)

    def at(lev_to, tile_to):
        return {"lev": lev_to, "tile": tile_to}

    def send(src, dst, send_sem, recv_sem, lev_to, tile_to):
        return pltpu.make_async_remote_copy(
            src_ref=src, dst_ref=dst, send_sem=send_sem, recv_sem=recv_sem,
            device_id=at(lev_to, tile_to), device_id_type=MESH,
        )

    def arrived(dst, sem):
        pltpu.make_async_copy(dst, dst, sem).wait()

    barrier = pltpu.get_barrier_semaphore()

    @pl.when(is_last)
    def _():
        pl.semaphore_wait(barrier, 4)
        for n in range(2):
            pl.semaphore_signal(near_sem, inc=1, device_id=at(lev_after - core + n, after), device_id_type=MESH)
        for n in range(2):
            pl.semaphore_signal(far_sem, inc=1, device_id=at(lev - core + n, after), device_id_type=MESH)

    for k in range(4):
        pl.semaphore_signal(barrier, inc=1, device_id=at(k, before), device_id_type=MESH)

    @pl.when(place < run - 2)
    def _():
        for k in range(4):
            pl.semaphore_signal(barrier, inc=1, device_id=at(k, after), device_id_type=MESH)

    @pl.when(jnp.logical_not(is_last))
    def _():
        for k in range(1, 4):
            pl.semaphore_signal(barrier, inc=1, device_id=at(lev ^ k, tile), device_id_type=MESH)

    small = [
        (courant.at[:, :, 0, :], cour), (upwind.at[:, :, 0, :], upw), (plume_in, plume), (control.at[:, 0, :], ctl),
        (mask_in, mask), (speed_in, speed), (factor_in, factor), (weight_in, weight), (profile_in, profile),
        (rate_in.at[:, 0, :], rate), (prec_in, prec),
    ]
    loads = [pltpu.make_async_copy(a, b, load_sem.at[n]) for n, (a, b) in enumerate(small)]
    for copy in loads:
        copy.start()

    def bg_copy(l):
        return pltpu.make_async_copy(background.at[:, l, 0, :], bg.at[l], bg_sem.at[l])

    def bg_start(l, _):
        bg_copy(l).start()
        return 0

    lax.fori_loop(0, nl, bg_start, 0)

    @pl.when(is_first)
    def _():
        pl.semaphore_wait(barrier, 7)

    @pl.when(jnp.logical_not(jnp.logical_or(is_first, is_last)))
    def _():
        pl.semaphore_wait(barrier, 11)

    @pl.when(place == run - 2)
    def _():
        for k in range(4):
            pl.semaphore_signal(entry_sem, inc=1, device_id=at(k, after), device_id_type=MESH)

    for n in range(3):
        loads[n].wait()
    plume_col = column(plume[...], nl)
    scaled = jnp.where(upw[...] == 1, cour[...], -cour[...]) * plume_col[None]
    face[0, own, :] = scaled[0]
    face[1, own, :] = scaled[1]
    face[2, own, :] = jnp.broadcast_to(plume_col, (nl, ny))
    for m in range(3):
        @pl.when(m < lev)
        def _():
            nface[m * nl:(m + 1) * nl, :] = jnp.zeros((nl, ny), F32)
    for n in range(3, 5):
        loads[n].wait()
    masked[0] = ctl[...] * mask[...].astype(F32)

    def upward(d):
        return pl.ds(d * nl, total - d * nl)

    def halo(d):
        return send(face.at[0, upward(d)], nface.at[upward(d)], halo_send.at[0], halo_recv.at[0], lev_before, before)

    def spread(k):
        return send(face.at[:, own], face.at[:, own], down_send.at[k], down_recv.at[lev], lev ^ k, tile)

    edges = [
        send(masked.at[0], edge.at[0], edge_send.at[0], edge_recv.at[0], lev_after, after),
        send(masked.at[0], edge.at[1], edge_send.at[1], edge_recv.at[1], lev_before, before),
    ]

    @pl.when(is_last)
    def _():
        edges[0].start()
        pl.semaphore_wait(entry_sem, 4)

    for k in range(1, 4):
        spread(k).start()

    @pl.when(jnp.logical_not(is_last))
    def _():
        edges[0].start()

    @pl.when(jnp.logical_not(is_first))
    def _():
        edges[1].start()

    for n in range(5, 11):
        loads[n].wait()
    row_i, lane_i = iota((nb, 128), 0), iota((nb, 128), 1)
    weight_row = pad_row(weight[...], 128)
    weight_col = column(weight_row, nb)
    shifted = jnp.broadcast_to(weight_row, (nb, 128))
    for bit in range(7):
        shifted = jnp.where((row_i >> bit) & 1 == 1, pltpu.roll(shifted, 128 - (1 << bit), 1), shifted)
    mixing = jnp.where(row_i + lane_i < nb, shifted, 0.0) - weight_row - weight_col
    mix_hi, mix_lo = split(jnp.where(lane_i < nb, mixing, 0.0))
    lhs[0:nb, 0:128] = mix_hi
    lhs[0:nb, 128:256] = mix_hi
    lhs[nb:2 * nb, 0:128] = mix_lo
    lhs[nb:2 * nb, 128:256] = jnp.zeros((nb, 128), BF16)

    speed_col = column(pad_row(speed[...], 128), nb)
    profile_col = column(pad_row(profile[...], 128), nb)
    factor_row = pad_row(factor[...], 128)
    fall = speed_col * factor_row
    above = fall / (1.0 + fall)
    fall = speed_col * pltpu.roll(jnp.broadcast_to(factor_row, (8, 128)), lax.rem(128 - lev * nl, 128), 1)[0:1]
    inverse = 1.0 / (1.0 + fall)
    gain = fall * inverse
    for l in range(nl):
        rb[l] = jnp.broadcast_to(inverse[:, l:l + 1], (nb, 128))
        gb[l] = jnp.broadcast_to(gain[:, l:l + 1], (nb, 128))
    chain = jnp.where(lane_i < (lev + 1) * nl, 1.0, above)
    step = 1
    while step < total:
        chain = chain * jnp.where(lane_i >= step, pltpu.roll(chain, step, 1), 1.0)
        step *= 2
    chain = jnp.where(lane_i < (lev + 1) * nl, 0.0, chain)[:, 0:total]

    masked[1] = pltpu.roll(masked[0], 1, 1)
    masked[2] = pltpu.roll(masked[0], ny - 1, 1)

    def mix_level(l, _):
        bg_copy(l).wait()
        hi, lo = split(bg[l])
        rest = jnp.zeros((128 - nb, ny), BF16)
        both = jnp.dot(lhs[...], jnp.concatenate([hi, rest, lo, rest], axis=0), preferred_element_type=F32)
        amp[l] = weight_col + rate[pl.ds(l, 1), :] * (both[0:nb] + both[nb:2 * nb])
        return 0

    lax.fori_loop(0, nl, mix_level, 0)

    def rows_of(c):
        return pl.ds(pl.multiple_of(c * chunk, 8), chunk)

    def wide(value):
        return jnp.concatenate([value] * (ny // 128), axis=1)

    rb[nl] = jnp.broadcast_to(profile_col, (nb, 128))

    def settle(c, _):
        rows = rows_of(c)
        value = jnp.zeros((chunk, ny), F32)
        for l in range(nl):
            value = amp[l, rows, :] * wide(rb[l, rows, :]) + value * wide(gb[l, rows, :])
            bfield[l, rows, :] = value
        return 0

    lax.fori_loop(0, 4, settle, 0)

    def faces():
        for k in range(1, 4):
            d = lev ^ k
            arrived(face.at[:, pl.ds(pl.multiple_of(d * nl, 8), nl)], down_recv.at[d])

    def send_halos():
        for d in range(4):
            @pl.when(d == lev_before)
            def _():
                halo(d).start()

    faces()

    @pl.when(jnp.logical_not(is_first))
    def _():
        send_halos()

    face_x, face_y = face[0], face[1]
    next_y = pltpu.roll(face_y, ny - 1, 1)
    coef[0] = jnp.maximum(face_y, 0.0)
    coef[1] = -jnp.minimum(next_y, 0.0)
    coef[2] = jnp.maximum(face_x, 0.0)
    coef[3] = face[2] + jnp.minimum(face_x, 0.0) + jnp.minimum(face_y, 0.0) - jnp.maximum(next_y, 0.0)
    for n in range(3):
        quot[n] = dot3(chain, coef[n])
        here[n] = coef[n, own, :]

    def others(c, t_sum):
        rows = rows_of(c)
        sums = [jnp.zeros((chunk, ny), F32) for _ in range(3)]
        for l in range(nl):
            value = bfield[l, rows, :]
            for n in range(3):
                sums[n] = sums[n] + value * here[n, l:l + 1, :]
        prof = wide(rb[nl, rows, :])
        value = bfield[nl - 1, rows, :]
        sums = [prof * (sums[n] + value * quot[n, rows, :]) for n in range(3)]
        kern[c, 0] = sums[0]
        kern[c, 1] = sums[1]
        kern[c, 3] = sums[2]
        part = masked[1, rows, :] * sums[0] + masked[2, rows, :] * sums[1]
        for r in range(0, chunk, 8):
            t_sum = t_sum + part[r:r + 8]
        return t_sum

    t_sum = lax.fori_loop(0, 4, others, jnp.zeros((8, ny), F32))

    @pl.when(is_first)
    def _():
        pl.semaphore_wait(near_sem, 2)
        send_halos()
        edges[1].start()
        pl.semaphore_wait(far_sem, 2)

    for d in range(4):
        @pl.when(d == lev)
        def _():
            arrived(nface.at[upward(d)], halo_recv.at[0])
    inflow = -jnp.minimum(nface[...], 0.0)
    ncoef[...] = inflow
    nhere[...] = ncoef[own, :]
    nquot[...] = dot3(chain, inflow)

    def right(c):
        return send(
            krow.at[rows_of(c)], right_in.at[0, core], right_send.at[c], right_recv.at[core], lev_after - core + c // 2, after
        )

    def right_both(c, to):
        return send(
            krow.at[rows_of(c)], right_in.at[1, lev], right_send.at[4 + 2 * (c // 2) + to // 2], right_recv.at[4 + lev],
            to + c // 2, after,
        )

    def next_row(i, _):
        c = lax.rem(2 * i, 4) + i // 2
        rows = rows_of(c)
        total_in = jnp.zeros((chunk, ny), F32)
        for l in range(nl):
            total_in = total_in + bfield[l, rows, :] * nhere[l:l + 1, :]
        krow[rows, :] = wide(rb[nl, rows, :]) * (total_in + bfield[nl - 1, rows, :] * nquot[rows, :])
        @pl.when(i < 2)
        def _():
            right(c).start()

        @pl.when(i >= 2)
        def _():
            for to in (0, 2):
                right_both(c, to).start()
        return 0

    lax.fori_loop(0, 4, next_row, 0)

    own_coef = coef[3] - jnp.maximum(nface[...], 0.0)
    coef[3] = own_coef
    quot[3] = dot3(chain, own_coef)
    here[3] = coef[3, own, :]

    def mine_to(c):
        return send(kern.at[c, pl.ds(0, 3)], mine_in.at[lev], mine_send.at[c], mine_recv.at[lev], c, tile)

    def left(c):
        return send(kern.at[c, 3], left_in.at[lev], left_send.at[c], left_recv.at[lev], c, before)

    def cell(c, t_sum):
        rows = rows_of(c)
        total_here = jnp.zeros((chunk, ny), F32)
        for l in range(nl):
            total_here = total_here + bfield[l, rows, :] * here[3, l:l + 1, :]
        total_here = wide(rb[nl, rows, :]) * (total_here + bfield[nl - 1, rows, :] * quot[3, rows, :])
        kern[c, 2] = total_here
        part = masked[0, rows, :] * total_here
        for r in range(0, chunk, 8):
            t_sum = t_sum + part[r:r + 8]
        return t_sum

    t_sum = lax.fori_loop(0, 4, cell, t_sum)

    def send_sums():
        for c in range(4):
            @pl.when(c != lev)
            def _():
                mine_to(c).start()
        for c in range(4):
            left(c).start()

    @pl.when(jnp.logical_not(is_last))
    def _():
        send_sums()

    for n in range(2):
        arrived(edge.at[n], edge_recv.at[n])
    for c in range(4):
        rows = pl.ds(c * chunk, chunk)
        part = edge[0, rows, :] * kern[c, 3] + edge[1, rows, :] * krow[rows, :]
        for r in range(0, chunk, 8):
            t_sum = t_sum + part[r:r + 8]
    t_mine = jnp.sum(t_sum, axis=0, keepdims=True) * scale
    s_mine = t_mine * prec[...] * scale
    t_own[...] = t_mine
    s_own[...] = s_mine

    t_sends = [send(s_own, t_left.at[lev], tx_send.at[k], tx_recv.at[lev], k, after) for k in range(4)]
    t_sends += [send(t_own, t_lev.at[k], tl_send.at[k], tl_recv.at[k], lev ^ k, tile) for k in range(1, 4)]
    t_sends += [send(s_own, t_right.at[lev], tx_send.at[4 + k], tx_recv.at[4 + lev], k, before) for k in range(4)]
    for copy in t_sends:
        copy.start()

    @pl.when(is_last)
    def _():
        send_sums()

    def part(n, k):
        return send(
            part_in.at[lev, n], part_in.at[lev, n], part_send.at[4 * n + k], part_recv.at[4 * n + lev], lev ^ k, tile
        )

    def from_before():
        for k in range(2):
            arrived(right_in.at[0, k], right_recv.at[k])
        part_in[lev, 0] = right_in[0, 0] + right_in[0, 1]
        for k in (2, 3, 1):
            part(0, k).start()
        for k in range(4):
            arrived(right_in.at[1, k], right_recv.at[4 + k])
        part_in[lev, 1] = (right_in[1, 0] + right_in[1, 1]) + (right_in[1, 2] + right_in[1, 3])
        part(1, 1).start()

    @pl.when(jnp.logical_not(is_first))
    def _():
        from_before()

    totals = [kern[lev, n] for n in range(3)]
    for k in range(1, 4):
        d = lev ^ k
        arrived(mine_in.at[d], mine_recv.at[d])
        totals = [totals[n] + mine_in[d, n] for n in range(3)]
    t_all = t_mine
    for k in range(1, 4):
        arrived(t_lev.at[k], tl_recv.at[k])
        t_all = t_all + t_lev[k]
    obs_out[...] = t_all
    s_here = t_all * prec[...] * scale
    result = totals[2] * s_here + pltpu.roll(totals[0] * s_here, ny - 1, 1) + pltpu.roll(totals[1] * s_here, 1, 1)
    for k in range(4):
        arrived(left_in.at[k], left_recv.at[k])
    from_after = (left_in[0] + left_in[1]) + (left_in[2] + left_in[3])
    for k in range(4):
        arrived(t_right.at[k], tx_recv.at[4 + k])
    s_after = (t_right[0] + t_right[1]) + (t_right[2] + t_right[3])
    mine = rows_of(lev)
    out_buf[mine, :] = result + from_after * s_after
    gathers = [
        send(out_buf.at[mine], out_buf.at[mine], ag_send.at[k], ag_recv.at[lev], lev ^ k, tile) for k in range(1, 4)
    ]
    for copy in gathers:
        copy.start()

    @pl.when(is_first)
    def _():
        from_before()

    for d in range(4):
        @pl.when(d == lev_before)
        def _():
            halo(d).wait_send()
    for k in range(1, 4):
        spread(k).wait_send()
    for h in range(2):
        right(2 * h).wait_send()
        for to in (0, 2):
            right_both(2 * h + 1, to).wait_send()
    for copy in edges + t_sends:
        copy.wait_send()
    for c in range(4):
        @pl.when(c != lev)
        def _():
            mine_to(c).wait_send()
        left(c).wait_send()

    for copy in gathers:
        copy.wait_send()

    for k in range(1, 4):
        d = lev ^ k
        arrived(out_buf.at[rows_of(d)], ag_recv.at[d])
    arrived(part_in.at[lev ^ 1, 1], part_recv.at[4 + (lev ^ 1)])
    for k in range(1, 4):
        d = lev ^ k
        arrived(part_in.at[d, 0], part_recv.at[d])
    for k in range(1, 4):
        part(0, k).wait_send()
    part(1, 1).wait_send()
    for k in range(4):
        arrived(t_left.at[k], tx_recv.at[k])
    s_before = (t_left[0] + t_left[1]) + (t_left[2] + t_left[3])
    mask_row = mask[...].astype(F32)
    for h in range(2):
        rows = pl.ds((2 * h + 1) * chunk, chunk)
        hess_out[rows, 0, :] = mask_row * (out_buf[rows, :] + part_in[lev - core + h, 1] * s_before)
        rows = pl.ds(2 * h * chunk, chunk)
        hess_out[rows, 0, :] = mask_row * (out_buf[rows, :] + (part_in[h, 0] + part_in[2 + h, 0]) * s_before)


def per_device(
    control, emit_mask, bin_profile, plume_profile, courant, upwind, bin_speed, level_factor, background, coag_rate,
    obs_weight, obs_precision,
):
    nb, nl, _, ny = background.shape
    total = level_factor.shape[0]
    chunk = nb // 4
    vmem, dma = pltpu.VMEM, pltpu.SemaphoreType.DMA
    obs, hess = pl.pallas_call(
        functools.partial(kernel, nb, nl, total, 1.0 / (nb * total)),
        out_shape=(jax.ShapeDtypeStruct((1, ny), F32), jax.ShapeDtypeStruct((nb, 1, ny), F32)),
        in_specs=[pl.BlockSpec(memory_space=pl.ANY)] * 12,
        out_specs=(pl.BlockSpec(memory_space=pltpu.VMEM),) * 2,
        scratch_shapes=[
            vmem((nl, nb, ny), F32),
            vmem((nb, ny), F32),
            vmem((1, ny), jnp.int32),
            vmem((1, nb), F32),
            vmem((1, nl), F32),
            vmem((2, nl, ny), F32),
            vmem((2, nl, ny), jnp.int32),
            vmem((1, nb), F32),
            vmem((1, total), F32),
            vmem((nl, ny), F32),
            vmem((1, nb), F32),
            vmem((1, ny), F32),
            vmem((2 * nb, 256), BF16),
            vmem((nl, nb, ny), F32),
            vmem((nl + 1, nb, 128), F32),
            vmem((nl, nb, 128), F32),
            vmem((nl, nb, ny), F32),
            vmem((3, total, ny), F32),
            vmem((total, ny), F32),
            vmem((4, total, ny), F32),
            vmem((total, ny), F32),
            vmem((4, nl, ny), F32),
            vmem((nl, ny), F32),
            vmem((4, nb, ny), F32),
            vmem((nb, ny), F32),
            vmem((3, nb, ny), F32),
            vmem((2, nb, ny), F32),
            vmem((4, 4, chunk, ny), F32),
            vmem((nb, ny), F32),
            vmem((4, 3, chunk, ny), F32),
            vmem((4, chunk, ny), F32),
            vmem((2, 4, chunk, ny), F32),
            vmem((4, 2, chunk, ny), F32),
            vmem((4, 1, ny), F32),
            vmem((4, 1, ny), F32),
            vmem((4, 1, ny), F32),
            vmem((1, ny), F32),
            vmem((1, ny), F32),
            vmem((nb, ny), F32),
            dma((11,)), dma((nl,)),
            dma((4,)), dma((4,)), dma((4,)), dma((4,)), dma((2,)), dma((2,)),
            dma((4,)), dma((4,)), dma((4,)), dma((4,)), dma((8,)), dma((8,)),
            dma((8,)), dma((8,)), dma((4,)), dma((4,)), dma((8,)), dma((8,)), dma((4,)), dma((4,)),
            pltpu.SemaphoreType.REGULAR, pltpu.SemaphoreType.REGULAR, pltpu.SemaphoreType.REGULAR,
        ],
        compiler_params=pltpu.CompilerParams(collective_id=0, has_side_effects=True, vmem_limit_bytes=24 << 20),
        name="hessian",
    )(*[
        pltpu.with_memory_space_constraint(value, pltpu.HBM) for value in (
            control, emit_mask, bin_profile[None], plume_profile[None], courant, upwind, bin_speed[None],
            level_factor[None], background, coag_rate, obs_weight[None], obs_precision,
        )
    ])
    return obs, hess


def solution(mesh):
    in_specs = (
        P(None, "tile", None), P("tile", None), P(), P("lev"), P(None, "lev", "tile", None), P(None, "lev", "tile", None),
        P(), P(), P(None, "lev", "tile", None), P("lev", "tile", None), P(), P("tile", None),
    )
    out_specs = (P("tile", None), P(None, "tile", None))
    return jax.shard_map(per_device, mesh=mesh, in_specs=in_specs, out_specs=out_specs, check_vma=False)
```

```python
import functools

import jax
import jax.numpy as jnp
from jax import lax
from jax.experimental import pallas as pl
from jax.experimental.pallas import tpu as pltpu
from jax.sharding import PartitionSpec as P

MESH = pl.DeviceIdType.MESH
F32, BF16 = jnp.float32, jnp.bfloat16


def split(value):
    high = value.astype(BF16)
    return high, (value - high.astype(F32)).astype(BF16)


def dot3(a, b):
    a_hi, a_lo = split(a)
    b_hi, b_lo = split(b)
    dot = functools.partial(jnp.dot, preferred_element_type=F32)
    return dot(a_hi, b_hi) + (dot(a_hi, b_lo) + dot(a_lo, b_hi))


def iota(shape, dim):
    return lax.broadcasted_iota(jnp.int32, shape, dim)


def pad_row(row, lanes):
    return jnp.concatenate([row, jnp.zeros((1, lanes - row.shape[1]), row.dtype)], axis=1)


def column(row, rows):
    shape = (rows, row.shape[1])
    picked = jnp.where(iota(shape, 0) == iota(shape, 1), jnp.broadcast_to(row, shape), 0.0)
    return jnp.sum(picked, axis=1, keepdims=True)


def kernel(
    nb, nl, total, scale,
    control, mask_in, profile_in, plume_in, courant, upwind, speed_in, factor_in, background, rate_in, weight_in, prec_in,
    obs_out, hess_out,
    bg, ctl, mask, profile, plume, cour, upw, speed, factor, rate, weight, prec,
    lhs, amp, rb, gb, bfield, face, nface, coef, ncoef, here, nhere, quot, nquot, masked, edge, kern,
    krow, mine_in, left_in, right_in, part_in, t_lev, t_left, t_right, t_own, s_own, out_buf,
    load_sem, bg_sem,
    halo_send, halo_recv, down_send, down_recv, edge_send, edge_recv,
    mine_send, mine_recv, left_send, left_recv, right_send, right_recv,
    part_send, part_recv, tl_send, tl_recv, tx_send, tx_recv, ag_send, ag_recv, near_sem, far_sem, entry_sem,
):
    lev, tile = lax.axis_index("lev"), lax.axis_index("tile")
    tiles = lax.axis_size("tile")
    before, after = lax.rem(tile + tiles - 1, tiles), lax.rem(tile + 1, tiles)
    ny = bg.shape[2]
    chunk = nb // 4
    run = min(8, tiles)
    place = lax.rem(tile, run)
    is_first, is_last = place == 0, place == run - 1
    lev_after = lev ^ jnp.where(is_last, 2, 0)
    lev_before = lev ^ jnp.where(is_first, 2, 0)
    core = lax.rem(lev, 2)
    own = pl.ds(pl.multiple_of(lev * nl, 8), nl)

    def at(lev_to, tile_to):
        return {"lev": lev_to, "tile": tile_to}

    def send(src, dst, send_sem, recv_sem, lev_to, tile_to):
        return pltpu.make_async_remote_copy(
            src_ref=src, dst_ref=dst, send_sem=send_sem, recv_sem=recv_sem,
            device_id=at(lev_to, tile_to), device_id_type=MESH,
        )

    def arrived(dst, sem):
        pltpu.make_async_copy(dst, dst, sem).wait()

    barrier = pltpu.get_barrier_semaphore()

    @pl.when(is_last)
    def _():
        pl.semaphore_wait(barrier, 4)
        for n in range(2):
            pl.semaphore_signal(near_sem, inc=1, device_id=at(lev_after - core + n, after), device_id_type=MESH)
        for n in range(2):
            pl.semaphore_signal(far_sem, inc=1, device_id=at(lev - core + n, after), device_id_type=MESH)

    for k in range(4):
        pl.semaphore_signal(barrier, inc=1, device_id=at(k, before), device_id_type=MESH)

    @pl.when(place < run - 2)
    def _():
        for k in range(4):
            pl.semaphore_signal(barrier, inc=1, device_id=at(k, after), device_id_type=MESH)

    @pl.when(jnp.logical_not(is_last))
    def _():
        for k in range(1, 4):
            pl.semaphore_signal(barrier, inc=1, device_id=at(lev ^ k, tile), device_id_type=MESH)

    small = [
        (courant.at[:, :, 0, :], cour), (upwind.at[:, :, 0, :], upw), (plume_in, plume), (control.at[:, 0, :], ctl),
        (mask_in, mask), (speed_in, speed), (factor_in, factor), (weight_in, weight), (profile_in, profile),
        (rate_in.at[:, 0, :], rate), (prec_in, prec),
    ]
    loads = [pltpu.make_async_copy(a, b, load_sem.at[n]) for n, (a, b) in enumerate(small)]
    for copy in loads:
        copy.start()

    def bg_copy(l):
        return pltpu.make_async_copy(background.at[:, l, 0, :], bg.at[l], bg_sem.at[l])

    def bg_start(l, _):
        bg_copy(l).start()
        return 0

    lax.fori_loop(0, nl, bg_start, 0)

    @pl.when(is_first)
    def _():
        pl.semaphore_wait(barrier, 7)

    @pl.when(jnp.logical_not(jnp.logical_or(is_first, is_last)))
    def _():
        pl.semaphore_wait(barrier, 11)

    @pl.when(place == run - 2)
    def _():
        for k in range(4):
            pl.semaphore_signal(entry_sem, inc=1, device_id=at(k, after), device_id_type=MESH)

    for n in range(3):
        loads[n].wait()
    plume_col = column(plume[...], nl)
    scaled = jnp.where(upw[...] == 1, cour[...], -cour[...]) * plume_col[None]
    face[0, own, :] = scaled[0]
    face[1, own, :] = scaled[1]
    face[2, own, :] = jnp.broadcast_to(plume_col, (nl, ny))
    for m in range(3):
        @pl.when(m < lev)
        def _():
            nface[m * nl:(m + 1) * nl, :] = jnp.zeros((nl, ny), F32)
    for n in range(3, 5):
        loads[n].wait()
    masked[0] = ctl[...] * mask[...].astype(F32)

    def upward(d):
        return pl.ds(d * nl, total - d * nl)

    def halo(d):
        return send(face.at[0, upward(d)], nface.at[upward(d)], halo_send.at[0], halo_recv.at[0], lev_before, before)

    def spread(k):
        return send(face.at[:, own], face.at[:, own], down_send.at[k], down_recv.at[lev], lev ^ k, tile)

    edges = [
        send(masked.at[0], edge.at[0], edge_send.at[0], edge_recv.at[0], lev_after, after),
        send(masked.at[0], edge.at[1], edge_send.at[1], edge_recv.at[1], lev_before, before),
    ]

    @pl.when(is_last)
    def _():
        edges[0].start()
        pl.semaphore_wait(entry_sem, 4)

    for k in range(1, 4):
        spread(k).start()

    @pl.when(jnp.logical_not(is_last))
    def _():
        edges[0].start()

    @pl.when(jnp.logical_not(is_first))
    def _():
        edges[1].start()

    for n in range(5, 11):
        loads[n].wait()
    row_i, lane_i = iota((nb, 128), 0), iota((nb, 128), 1)
    weight_row = pad_row(weight[...], 128)
    weight_col = column(weight_row, nb)
    shifted = jnp.broadcast_to(weight_row, (nb, 128))
    for bit in range(7):
        shifted = jnp.where((row_i >> bit) & 1 == 1, pltpu.roll(shifted, 128 - (1 << bit), 1), shifted)
    mixing = jnp.where(row_i + lane_i < nb, shifted, 0.0) - weight_row - weight_col
    mix_hi, mix_lo = split(jnp.where(lane_i < nb, mixing, 0.0))
    lhs[0:nb, 0:128] = mix_hi
    lhs[0:nb, 128:256] = mix_hi
    lhs[nb:2 * nb, 0:128] = mix_lo
    lhs[nb:2 * nb, 128:256] = jnp.zeros((nb, 128), BF16)

    speed_col = column(pad_row(speed[...], 128), nb)
    profile_col = column(pad_row(profile[...], 128), nb)
    factor_row = pad_row(factor[...], 128)
    fall = speed_col * factor_row
    above = fall / (1.0 + fall)
    fall = speed_col * pltpu.roll(jnp.broadcast_to(factor_row, (8, 128)), lax.rem(128 - lev * nl, 128), 1)[0:1]
    inverse = 1.0 / (1.0 + fall)
    gain = fall * inverse
    for l in range(nl):
        rb[l] = jnp.broadcast_to(inverse[:, l:l + 1], (nb, 128))
        gb[l] = jnp.broadcast_to(gain[:, l:l + 1], (nb, 128))
    chain = jnp.where(lane_i < (lev + 1) * nl, 1.0, above)
    step = 1
    while step < total:
        chain = chain * jnp.where(lane_i >= step, pltpu.roll(chain, step, 1), 1.0)
        step *= 2
    chain = jnp.where(lane_i < (lev + 1) * nl, 0.0, chain)[:, 0:total]

    masked[1] = pltpu.roll(masked[0], 1, 1)
    masked[2] = pltpu.roll(masked[0], ny - 1, 1)

    def mix_level(l, _):
        bg_copy(l).wait()
        hi, lo = split(bg[l])
        rest = jnp.zeros((128 - nb, ny), BF16)
        both = jnp.dot(lhs[...], jnp.concatenate([hi, rest, lo, rest], axis=0), preferred_element_type=F32)
        amp[l] = weight_col + rate[pl.ds(l, 1), :] * (both[0:nb] + both[nb:2 * nb])
        return 0

    lax.fori_loop(0, nl, mix_level, 0)

    def rows_of(c):
        return pl.ds(pl.multiple_of(c * chunk, 8), chunk)

    def wide(value):
        return jnp.concatenate([value] * (ny // 128), axis=1)

    rb[nl] = jnp.broadcast_to(profile_col, (nb, 128))

    def settle(c, _):
        rows = rows_of(c)
        value = jnp.zeros((chunk, ny), F32)
        for l in range(nl):
            value = amp[l, rows, :] * wide(rb[l, rows, :]) + value * wide(gb[l, rows, :])
            bfield[l, rows, :] = value
        return 0

    lax.fori_loop(0, 4, settle, 0)

    def faces():
        for k in range(1, 4):
            d = lev ^ k
            arrived(face.at[:, pl.ds(pl.multiple_of(d * nl, 8), nl)], down_recv.at[d])

    def send_halos():
        for d in range(4):
            @pl.when(d == lev_before)
            def _():
                halo(d).start()

    faces()

    @pl.when(jnp.logical_not(is_first))
    def _():
        send_halos()

    face_x, face_y = face[0], face[1]
    next_y = pltpu.roll(face_y, ny - 1, 1)
    coef[0] = jnp.maximum(face_y, 0.0)
    coef[1] = -jnp.minimum(next_y, 0.0)
    coef[2] = jnp.maximum(face_x, 0.0)
    coef[3] = face[2] + jnp.minimum(face_x, 0.0) + jnp.minimum(face_y, 0.0) - jnp.maximum(next_y, 0.0)
    for n in range(3):
        quot[n] = dot3(chain, coef[n])
        here[n] = coef[n, own, :]

    def others(c, t_sum):
        rows = rows_of(c)
        sums = [jnp.zeros((chunk, ny), F32) for _ in range(3)]
        for l in range(nl):
            value = bfield[l, rows, :]
            for n in range(3):
                sums[n] = sums[n] + value * here[n, l:l + 1, :]
        prof = wide(rb[nl, rows, :])
        value = bfield[nl - 1, rows, :]
        sums = [prof * (sums[n] + value * quot[n, rows, :]) for n in range(3)]
        kern[c, 0] = sums[0]
        kern[c, 1] = sums[1]
        kern[c, 3] = sums[2]
        part = masked[1, rows, :] * sums[0] + masked[2, rows, :] * sums[1]
        for r in range(0, chunk, 8):
            t_sum = t_sum + part[r:r + 8]
        return t_sum

    t_sum = lax.fori_loop(0, 4, others, jnp.zeros((8, ny), F32))

    @pl.when(is_first)
    def _():
        pl.semaphore_wait(near_sem, 2)
        send_halos()
        edges[1].start()
        pl.semaphore_wait(far_sem, 2)

    for d in range(4):
        @pl.when(d == lev)
        def _():
            arrived(nface.at[upward(d)], halo_recv.at[0])
    inflow = -jnp.minimum(nface[...], 0.0)
    ncoef[...] = inflow
    nhere[...] = ncoef[own, :]
    nquot[...] = dot3(chain, inflow)

    def right(c):
        return send(
            krow.at[rows_of(c)], right_in.at[0, core], right_send.at[c], right_recv.at[core], lev_after - core + c // 2, after
        )

    def right_both(c, to):
        return send(
            krow.at[rows_of(c)], right_in.at[1, lev], right_send.at[4 + 2 * (c // 2) + to // 2], right_recv.at[4 + lev],
            to + c // 2, after,
        )

    def next_row(i, _):
        c = lax.rem(2 * i, 4) + i // 2
        rows = rows_of(c)
        total_in = jnp.zeros((chunk, ny), F32)
        for l in range(nl):
            total_in = total_in + bfield[l, rows, :] * nhere[l:l + 1, :]
        krow[rows, :] = wide(rb[nl, rows, :]) * (total_in + bfield[nl - 1, rows, :] * nquot[rows, :])
        @pl.when(i < 2)
        def _():
            right(c).start()

        @pl.when(i >= 2)
        def _():
            for to in (0, 2):
                right_both(c, to).start()
        return 0

    lax.fori_loop(0, 4, next_row, 0)

    own_coef = coef[3] - jnp.maximum(nface[...], 0.0)
    coef[3] = own_coef
    quot[3] = dot3(chain, own_coef)
    here[3] = coef[3, own, :]

    def mine_to(c):
        return send(kern.at[c, pl.ds(0, 3)], mine_in.at[lev], mine_send.at[c], mine_recv.at[lev], c, tile)

    def left(c):
        return send(kern.at[c, 3], left_in.at[lev], left_send.at[c], left_recv.at[lev], c, before)

    def cell(c, t_sum):
        rows = rows_of(c)
        total_here = jnp.zeros((chunk, ny), F32)
        for l in range(nl):
            total_here = total_here + bfield[l, rows, :] * here[3, l:l + 1, :]
        total_here = wide(rb[nl, rows, :]) * (total_here + bfield[nl - 1, rows, :] * quot[3, rows, :])
        kern[c, 2] = total_here
        part = masked[0, rows, :] * total_here
        for r in range(0, chunk, 8):
            t_sum = t_sum + part[r:r + 8]
        return t_sum

    t_sum = lax.fori_loop(0, 4, cell, t_sum)

    def send_sums():
        for c in range(4):
            @pl.when(c != lev)
            def _():
                mine_to(c).start()
        for c in range(4):
            left(c).start()

    @pl.when(jnp.logical_not(is_last))
    def _():
        send_sums()

    for n in range(2):
        arrived(edge.at[n], edge_recv.at[n])
    for c in range(4):
        rows = pl.ds(c * chunk, chunk)
        part = edge[0, rows, :] * kern[c, 3] + edge[1, rows, :] * krow[rows, :]
        for r in range(0, chunk, 8):
            t_sum = t_sum + part[r:r + 8]
    t_mine = jnp.sum(t_sum, axis=0, keepdims=True) * scale
    s_mine = t_mine * prec[...] * scale
    t_own[...] = t_mine
    s_own[...] = s_mine

    t_sends = [
        send(s_own, t_left.at[lev], tx_send.at[k], tx_recv.at[lev], 2 - lev_after + core + k if k < 2 else lev_after - core + k - 2, after)
        for k in range(4)
    ]
    t_sends += [send(t_own, t_lev.at[k], tl_send.at[k], tl_recv.at[k], lev ^ k, tile) for k in range(1, 4)]
    t_sends += [send(s_own, t_right.at[lev], tx_send.at[4 + k], tx_recv.at[4 + lev], k, before) for k in range(4)]
    for copy in t_sends:
        copy.start()

    @pl.when(is_last)
    def _():
        send_sums()

    def part(n, k):
        return send(
            part_in.at[lev, n], part_in.at[lev, n], part_send.at[4 * n + k], part_recv.at[4 * n + lev], lev ^ k, tile
        )

    def from_before():
        for k in range(2):
            arrived(right_in.at[0, k], right_recv.at[k])
        part_in[lev, 0] = right_in[0, 0] + right_in[0, 1]
        for k in (2, 3, 1):
            part(0, k).start()
        for k in range(4):
            arrived(right_in.at[1, k], right_recv.at[4 + k])
        part_in[lev, 1] = (right_in[1, 0] + right_in[1, 1]) + (right_in[1, 2] + right_in[1, 3])
        part(1, 1).start()

    @pl.when(jnp.logical_not(is_first))
    def _():
        from_before()

    totals = [kern[lev, n] for n in range(3)]
    for k in range(1, 4):
        d = lev ^ k
        arrived(mine_in.at[d], mine_recv.at[d])
        totals = [totals[n] + mine_in[d, n] for n in range(3)]
    t_all = t_mine
    for k in range(1, 4):
        arrived(t_lev.at[k], tl_recv.at[k])
        t_all = t_all + t_lev[k]
    obs_out[...] = t_all
    s_here = t_all * prec[...] * scale
    result = totals[2] * s_here + pltpu.roll(totals[0] * s_here, ny - 1, 1) + pltpu.roll(totals[1] * s_here, 1, 1)
    for k in range(4):
        arrived(left_in.at[k], left_recv.at[k])
    from_after = (left_in[0] + left_in[1]) + (left_in[2] + left_in[3])
    for k in range(4):
        arrived(t_right.at[k], tx_recv.at[4 + k])
    s_after = (t_right[0] + t_right[1]) + (t_right[2] + t_right[3])
    mine = rows_of(lev)
    out_buf[mine, :] = result + from_after * s_after
    gathers = [
        send(out_buf.at[mine], out_buf.at[mine], ag_send.at[k], ag_recv.at[lev], lev ^ k, tile) for k in range(1, 4)
    ]
    for copy in gathers:
        copy.start()

    @pl.when(is_first)
    def _():
        from_before()

    for d in range(4):
        @pl.when(d == lev_before)
        def _():
            halo(d).wait_send()
    for k in range(1, 4):
        spread(k).wait_send()
    for h in range(2):
        right(2 * h).wait_send()
        for to in (0, 2):
            right_both(2 * h + 1, to).wait_send()
    for copy in edges + t_sends:
        copy.wait_send()
    for c in range(4):
        @pl.when(c != lev)
        def _():
            mine_to(c).wait_send()
        left(c).wait_send()

    for copy in gathers:
        copy.wait_send()

    for k in range(1, 4):
        d = lev ^ k
        arrived(out_buf.at[rows_of(d)], ag_recv.at[d])
    arrived(part_in.at[lev ^ 1, 1], part_recv.at[4 + (lev ^ 1)])
    part(1, 1).wait_send()
    for k in range(4):
        arrived(t_left.at[k], tx_recv.at[k])
    s_before = (t_left[0] + t_left[1]) + (t_left[2] + t_left[3])
    mask_row = mask[...].astype(F32)
    for h in range(2):
        rows = pl.ds((2 * h + 1) * chunk, chunk)
        hess_out[rows, 0, :] = mask_row * (out_buf[rows, :] + part_in[lev - core + h, 1] * s_before)
    for k in range(1, 4):
        part(0, k).wait_send()
    for k in range(1, 4):
        d = lev ^ k
        arrived(part_in.at[d, 0], part_recv.at[d])
    for h in range(2):
        rows = pl.ds(2 * h * chunk, chunk)
        hess_out[rows, 0, :] = mask_row * (out_buf[rows, :] + (part_in[h, 0] + part_in[2 + h, 0]) * s_before)


def per_device(
    control, emit_mask, bin_profile, plume_profile, courant, upwind, bin_speed, level_factor, background, coag_rate,
    obs_weight, obs_precision,
):
    nb, nl, _, ny = background.shape
    total = level_factor.shape[0]
    chunk = nb // 4
    vmem, dma = pltpu.VMEM, pltpu.SemaphoreType.DMA
    obs, hess = pl.pallas_call(
        functools.partial(kernel, nb, nl, total, 1.0 / (nb * total)),
        out_shape=(jax.ShapeDtypeStruct((1, ny), F32), jax.ShapeDtypeStruct((nb, 1, ny), F32)),
        in_specs=[pl.BlockSpec(memory_space=pl.ANY)] * 12,
        out_specs=(pl.BlockSpec(memory_space=pltpu.VMEM),) * 2,
        scratch_shapes=[
            vmem((nl, nb, ny), F32),
            vmem((nb, ny), F32),
            vmem((1, ny), jnp.int32),
            vmem((1, nb), F32),
            vmem((1, nl), F32),
            vmem((2, nl, ny), F32),
            vmem((2, nl, ny), jnp.int32),
            vmem((1, nb), F32),
            vmem((1, total), F32),
            vmem((nl, ny), F32),
            vmem((1, nb), F32),
            vmem((1, ny), F32),
            vmem((2 * nb, 256), BF16),
            vmem((nl, nb, ny), F32),
            vmem((nl + 1, nb, 128), F32),
            vmem((nl, nb, 128), F32),
            vmem((nl, nb, ny), F32),
            vmem((3, total, ny), F32),
            vmem((total, ny), F32),
            vmem((4, total, ny), F32),
            vmem((total, ny), F32),
            vmem((4, nl, ny), F32),
            vmem((nl, ny), F32),
            vmem((4, nb, ny), F32),
            vmem((nb, ny), F32),
            vmem((3, nb, ny), F32),
            vmem((2, nb, ny), F32),
            vmem((4, 4, chunk, ny), F32),
            vmem((nb, ny), F32),
            vmem((4, 3, chunk, ny), F32),
            vmem((4, chunk, ny), F32),
            vmem((2, 4, chunk, ny), F32),
            vmem((4, 2, chunk, ny), F32),
            vmem((4, 1, ny), F32),
            vmem((4, 1, ny), F32),
            vmem((4, 1, ny), F32),
            vmem((1, ny), F32),
            vmem((1, ny), F32),
            vmem((nb, ny), F32),
            dma((11,)), dma((nl,)),
            dma((4,)), dma((4,)), dma((4,)), dma((4,)), dma((2,)), dma((2,)),
            dma((4,)), dma((4,)), dma((4,)), dma((4,)), dma((8,)), dma((8,)),
            dma((8,)), dma((8,)), dma((4,)), dma((4,)), dma((8,)), dma((8,)), dma((4,)), dma((4,)),
            pltpu.SemaphoreType.REGULAR, pltpu.SemaphoreType.REGULAR, pltpu.SemaphoreType.REGULAR,
        ],
        compiler_params=pltpu.CompilerParams(collective_id=0, has_side_effects=True, vmem_limit_bytes=24 << 20),
        name="hessian",
    )(*[
        pltpu.with_memory_space_constraint(value, pltpu.HBM) for value in (
            control, emit_mask, bin_profile[None], plume_profile[None], courant, upwind, bin_speed[None],
            level_factor[None], background, coag_rate, obs_weight[None], obs_precision,
        )
    ])
    return obs, hess


def solution(mesh):
    in_specs = (
        P(None, "tile", None), P("tile", None), P(), P("lev"), P(None, "lev", "tile", None), P(None, "lev", "tile", None),
        P(), P(), P(None, "lev", "tile", None), P("lev", "tile", None), P(), P("tile", None),
    )
    out_specs = (P("tile", None), P(None, "tile", None))
    return jax.shard_map(per_device, mesh=mesh, in_specs=in_specs, out_specs=out_specs, check_vma=False)
```

```python
import functools

import jax
import jax.numpy as jnp
from jax import lax
from jax.experimental import pallas as pl
from jax.experimental.pallas import tpu as pltpu
from jax.sharding import PartitionSpec as P

MESH = pl.DeviceIdType.MESH
F32, BF16 = jnp.float32, jnp.bfloat16


def split(value):
    high = value.astype(BF16)
    return high, (value - high.astype(F32)).astype(BF16)


def dot3(a, b):
    a_hi, a_lo = split(a)
    b_hi, b_lo = split(b)
    dot = functools.partial(jnp.dot, preferred_element_type=F32)
    return dot(a_hi, b_hi) + (dot(a_hi, b_lo) + dot(a_lo, b_hi))


def iota(shape, dim):
    return lax.broadcasted_iota(jnp.int32, shape, dim)


def pad_row(row, lanes):
    return jnp.concatenate([row, jnp.zeros((1, lanes - row.shape[1]), row.dtype)], axis=1)


def column(row, rows):
    shape = (rows, row.shape[1])
    picked = jnp.where(iota(shape, 0) == iota(shape, 1), jnp.broadcast_to(row, shape), 0.0)
    return jnp.sum(picked, axis=1, keepdims=True)


def kernel(
    nb, nl, total, scale,
    control, mask_in, profile_in, plume_in, courant, upwind, speed_in, factor_in, background, rate_in, weight_in, prec_in,
    obs_out, hess_out,
    bg, ctl, mask, profile, plume, cour, upw, speed, factor, rate, weight, prec,
    lhs, amp, rb, gb, bfield, face, nface, coef, ncoef, here, nhere, quot, nquot, masked, edge, kern,
    krow, mine_in, left_in, right_in, part_in, t_lev, t_left, t_right, t_own, s_own, out_buf,
    load_sem, bg_sem,
    halo_send, halo_recv, down_send, down_recv, edge_send, edge_recv,
    mine_send, mine_recv, left_send, left_recv, right_send, right_recv,
    part_send, part_recv, tl_send, tl_recv, tx_send, tx_recv, ag_send, ag_recv, near_sem, far_sem, entry_sem,
):
    lev, tile = lax.axis_index("lev"), lax.axis_index("tile")
    tiles = lax.axis_size("tile")
    before, after = lax.rem(tile + tiles - 1, tiles), lax.rem(tile + 1, tiles)
    ny = bg.shape[2]
    chunk = nb // 4
    run = min(8, tiles)
    place = lax.rem(tile, run)
    is_first, is_last = place == 0, place == run - 1
    lev_after = lev ^ jnp.where(is_last, 2, 0)
    lev_before = lev ^ jnp.where(is_first, 2, 0)
    core = lax.rem(lev, 2)
    own = pl.ds(pl.multiple_of(lev * nl, 8), nl)

    def at(lev_to, tile_to):
        return {"lev": lev_to, "tile": tile_to}

    def send(src, dst, send_sem, recv_sem, lev_to, tile_to):
        return pltpu.make_async_remote_copy(
            src_ref=src, dst_ref=dst, send_sem=send_sem, recv_sem=recv_sem,
            device_id=at(lev_to, tile_to), device_id_type=MESH,
        )

    def arrived(dst, sem):
        pltpu.make_async_copy(dst, dst, sem).wait()

    barrier = pltpu.get_barrier_semaphore()

    @pl.when(is_last)
    def _():
        pl.semaphore_wait(barrier, 4)
        for n in range(2):
            pl.semaphore_signal(near_sem, inc=1, device_id=at(lev_after - core + n, after), device_id_type=MESH)
        for n in range(2):
            pl.semaphore_signal(far_sem, inc=1, device_id=at(lev - core + n, after), device_id_type=MESH)

    for k in range(4):
        pl.semaphore_signal(barrier, inc=1, device_id=at(k, before), device_id_type=MESH)

    @pl.when(place < run - 2)
    def _():
        for k in range(4):
            pl.semaphore_signal(barrier, inc=1, device_id=at(k, after), device_id_type=MESH)

    @pl.when(jnp.logical_not(is_last))
    def _():
        for k in range(1, 4):
            pl.semaphore_signal(barrier, inc=1, device_id=at(lev ^ k, tile), device_id_type=MESH)

    small = [
        (courant.at[:, :, 0, :], cour), (upwind.at[:, :, 0, :], upw), (plume_in, plume), (control.at[:, 0, :], ctl),
        (mask_in, mask), (speed_in, speed), (factor_in, factor), (weight_in, weight), (profile_in, profile),
        (rate_in.at[:, 0, :], rate), (prec_in, prec),
    ]
    loads = [pltpu.make_async_copy(a, b, load_sem.at[n]) for n, (a, b) in enumerate(small)]
    for copy in loads:
        copy.start()

    def bg_copy(l):
        return pltpu.make_async_copy(background.at[:, l, 0, :], bg.at[l], bg_sem.at[l])

    def bg_start(l, _):
        bg_copy(l).start()
        return 0

    lax.fori_loop(0, nl, bg_start, 0)

    @pl.when(is_first)
    def _():
        pl.semaphore_wait(barrier, 7)

    @pl.when(jnp.logical_not(jnp.logical_or(is_first, is_last)))
    def _():
        pl.semaphore_wait(barrier, 11)

    @pl.when(place == run - 2)
    def _():
        for k in range(4):
            pl.semaphore_signal(entry_sem, inc=1, device_id=at(k, after), device_id_type=MESH)

    for n in range(3):
        loads[n].wait()
    plume_col = column(plume[...], nl)
    scaled = jnp.where(upw[...] == 1, cour[...], -cour[...]) * plume_col[None]
    face[0, own, :] = scaled[0]
    face[1, own, :] = scaled[1]
    face[2, own, :] = jnp.broadcast_to(plume_col, (nl, ny))
    for m in range(3):
        @pl.when(m < lev)
        def _():
            nface[m * nl:(m + 1) * nl, :] = jnp.zeros((nl, ny), F32)
    for n in range(3, 5):
        loads[n].wait()
    masked[0] = ctl[...] * mask[...].astype(F32)

    def upward(d):
        return pl.ds(d * nl, total - d * nl)

    def halo(d):
        return send(face.at[0, upward(d)], nface.at[upward(d)], halo_send.at[0], halo_recv.at[0], lev_before, before)

    def spread(k):
        return send(face.at[:, own], face.at[:, own], down_send.at[k], down_recv.at[lev], lev ^ k, tile)

    edges = [
        send(masked.at[0], edge.at[0], edge_send.at[0], edge_recv.at[0], lev_after, after),
        send(masked.at[0], edge.at[1], edge_send.at[1], edge_recv.at[1], lev_before, before),
    ]

    @pl.when(is_last)
    def _():
        edges[0].start()
        pl.semaphore_wait(entry_sem, 4)

    for k in range(1, 4):
        spread(k).start()

    @pl.when(jnp.logical_not(is_last))
    def _():
        edges[0].start()

    @pl.when(jnp.logical_not(is_first))
    def _():
        edges[1].start()

    for n in range(5, 11):
        loads[n].wait()
    row_i, lane_i = iota((nb, 128), 0), iota((nb, 128), 1)
    weight_row = pad_row(weight[...], 128)
    weight_col = column(weight_row, nb)
    shifted = jnp.broadcast_to(weight_row, (nb, 128))
    for bit in range(7):
        shifted = jnp.where((row_i >> bit) & 1 == 1, pltpu.roll(shifted, 128 - (1 << bit), 1), shifted)
    mixing = jnp.where(row_i + lane_i < nb, shifted, 0.0) - weight_row - weight_col
    mix_hi, mix_lo = split(jnp.where(lane_i < nb, mixing, 0.0))
    lhs[0:nb, 0:128] = mix_hi
    lhs[0:nb, 128:256] = mix_hi
    lhs[nb:2 * nb, 0:128] = mix_lo
    lhs[nb:2 * nb, 128:256] = jnp.zeros((nb, 128), BF16)

    speed_col = column(pad_row(speed[...], 128), nb)
    profile_col = column(pad_row(profile[...], 128), nb)
    factor_row = pad_row(factor[...], 128)
    fall = speed_col * factor_row
    above = fall / (1.0 + fall)
    fall = speed_col * pltpu.roll(jnp.broadcast_to(factor_row, (8, 128)), lax.rem(128 - lev * nl, 128), 1)[0:1]
    inverse = 1.0 / (1.0 + fall)
    gain = fall * inverse
    for l in range(nl):
        rb[l] = jnp.broadcast_to(inverse[:, l:l + 1], (nb, 128))
        gb[l] = jnp.broadcast_to(gain[:, l:l + 1], (nb, 128))
    chain = jnp.where(lane_i < (lev + 1) * nl, 1.0, above)
    step = 1
    while step < total:
        chain = chain * jnp.where(lane_i >= step, pltpu.roll(chain, step, 1), 1.0)
        step *= 2
    chain = jnp.where(lane_i < (lev + 1) * nl, 0.0, chain)[:, 0:total]

    masked[1] = pltpu.roll(masked[0], 1, 1)
    masked[2] = pltpu.roll(masked[0], ny - 1, 1)

    def mix_level(l, _):
        bg_copy(l).wait()
        hi, lo = split(bg[l])
        rest = jnp.zeros((128 - nb, ny), BF16)
        both = jnp.dot(lhs[...], jnp.concatenate([hi, rest, lo, rest], axis=0), preferred_element_type=F32)
        amp[l] = weight_col + rate[pl.ds(l, 1), :] * (both[0:nb] + both[nb:2 * nb])
        return 0

    lax.fori_loop(0, nl, mix_level, 0)

    def rows_of(c):
        return pl.ds(pl.multiple_of(c * chunk, 8), chunk)

    def wide(value):
        return jnp.concatenate([value] * (ny // 128), axis=1)

    rb[nl] = jnp.broadcast_to(profile_col, (nb, 128))

    def settle(c, _):
        rows = rows_of(c)
        value = jnp.zeros((chunk, ny), F32)
        for l in range(nl):
            value = amp[l, rows, :] * wide(rb[l, rows, :]) + value * wide(gb[l, rows, :])
            bfield[l, rows, :] = value
        return 0

    lax.fori_loop(0, 4, settle, 0)

    def faces():
        for k in range(1, 4):
            d = lev ^ k
            arrived(face.at[:, pl.ds(pl.multiple_of(d * nl, 8), nl)], down_recv.at[d])

    def send_halos():
        for d in range(4):
            @pl.when(d == lev_before)
            def _():
                halo(d).start()

    faces()

    @pl.when(jnp.logical_not(is_first))
    def _():
        send_halos()

    face_x, face_y = face[0], face[1]
    next_y = pltpu.roll(face_y, ny - 1, 1)
    coef[0] = jnp.maximum(face_y, 0.0)
    coef[1] = -jnp.minimum(next_y, 0.0)
    coef[2] = jnp.maximum(face_x, 0.0)
    coef[3] = face[2] + jnp.minimum(face_x, 0.0) + jnp.minimum(face_y, 0.0) - jnp.maximum(next_y, 0.0)
    for n in range(3):
        quot[n] = dot3(chain, coef[n])
        here[n] = coef[n, own, :]

    def others(c, t_sum):
        rows = rows_of(c)
        sums = [jnp.zeros((chunk, ny), F32) for _ in range(3)]
        for l in range(nl):
            value = bfield[l, rows, :]
            for n in range(3):
                sums[n] = sums[n] + value * here[n, l:l + 1, :]
        prof = wide(rb[nl, rows, :])
        value = bfield[nl - 1, rows, :]
        sums = [prof * (sums[n] + value * quot[n, rows, :]) for n in range(3)]
        kern[c, 0] = sums[0]
        kern[c, 1] = sums[1]
        kern[c, 3] = sums[2]
        part = masked[1, rows, :] * sums[0] + masked[2, rows, :] * sums[1]
        for r in range(0, chunk, 8):
            t_sum = t_sum + part[r:r + 8]
        return t_sum

    t_sum = lax.fori_loop(0, 4, others, jnp.zeros((8, ny), F32))

    @pl.when(is_first)
    def _():
        pl.semaphore_wait(near_sem, 2)
        send_halos()
        pl.semaphore_wait(far_sem, 2)
        edges[1].start()

    for d in range(4):
        @pl.when(d == lev)
        def _():
            arrived(nface.at[upward(d)], halo_recv.at[0])
    inflow = -jnp.minimum(nface[...], 0.0)
    ncoef[...] = inflow
    nhere[...] = ncoef[own, :]
    nquot[...] = dot3(chain, inflow)

    def right(c):
        return send(
            krow.at[rows_of(c)], right_in.at[0, core], right_send.at[c], right_recv.at[core], lev_after - core + c // 2, after
        )

    def right_both(c, to):
        return send(
            krow.at[rows_of(c)], right_in.at[1, lev], right_send.at[4 + 2 * (c // 2) + to // 2], right_recv.at[4 + lev],
            to + c // 2, after,
        )

    def next_row(i, _):
        c = lax.rem(2 * i, 4) + i // 2
        rows = rows_of(c)
        total_in = jnp.zeros((chunk, ny), F32)
        for l in range(nl):
            total_in = total_in + bfield[l, rows, :] * nhere[l:l + 1, :]
        krow[rows, :] = wide(rb[nl, rows, :]) * (total_in + bfield[nl - 1, rows, :] * nquot[rows, :])
        @pl.when(i < 2)
        def _():
            right(c).start()

        @pl.when(i >= 2)
        def _():
            for to in (0, 2):
                right_both(c, to).start()
        return 0

    lax.fori_loop(0, 4, next_row, 0)

    own_coef = coef[3] - jnp.maximum(nface[...], 0.0)
    coef[3] = own_coef
    quot[3] = dot3(chain, own_coef)
    here[3] = coef[3, own, :]

    def mine_to(c):
        return send(kern.at[c, pl.ds(0, 3)], mine_in.at[lev], mine_send.at[c], mine_recv.at[lev], c, tile)

    def left(c):
        return send(kern.at[c, 3], left_in.at[lev], left_send.at[c], left_recv.at[lev], c, before)

    def cell(c, t_sum):
        rows = rows_of(c)
        total_here = jnp.zeros((chunk, ny), F32)
        for l in range(nl):
            total_here = total_here + bfield[l, rows, :] * here[3, l:l + 1, :]
        total_here = wide(rb[nl, rows, :]) * (total_here + bfield[nl - 1, rows, :] * quot[3, rows, :])
        kern[c, 2] = total_here
        part = masked[0, rows, :] * total_here
        for r in range(0, chunk, 8):
            t_sum = t_sum + part[r:r + 8]
        return t_sum

    t_sum = lax.fori_loop(0, 4, cell, t_sum)

    def send_sums():
        for c in range(4):
            @pl.when(c != lev)
            def _():
                mine_to(c).start()
        for c in range(4):
            left(c).start()

    @pl.when(jnp.logical_not(is_last))
    def _():
        send_sums()

    for n in range(2):
        arrived(edge.at[n], edge_recv.at[n])
    for c in range(4):
        rows = pl.ds(c * chunk, chunk)
        part = edge[0, rows, :] * kern[c, 3] + edge[1, rows, :] * krow[rows, :]
        for r in range(0, chunk, 8):
            t_sum = t_sum + part[r:r + 8]
    t_mine = jnp.sum(t_sum, axis=0, keepdims=True) * scale
    s_mine = t_mine * prec[...] * scale
    t_own[...] = t_mine
    s_own[...] = s_mine

    t_sends = [send(s_own, t_left.at[lev], tx_send.at[k], tx_recv.at[lev], k, after) for k in range(4)]
    t_sends += [send(t_own, t_lev.at[k], tl_send.at[k], tl_recv.at[k], lev ^ k, tile) for k in range(1, 4)]
    t_sends += [send(s_own, t_right.at[lev], tx_send.at[4 + k], tx_recv.at[4 + lev], k, before) for k in range(4)]
    for copy in t_sends:
        copy.start()

    @pl.when(is_last)
    def _():
        send_sums()

    def part(n, k):
        return send(
            part_in.at[lev, n], part_in.at[lev, n], part_send.at[4 * n + k], part_recv.at[4 * n + lev], lev ^ k, tile
        )

    def from_before():
        for k in range(2):
            arrived(right_in.at[0, k], right_recv.at[k])
        part_in[lev, 0] = right_in[0, 0] + right_in[0, 1]
        for k in (2, 3, 1):
            part(0, k).start()
        for k in range(4):
            arrived(right_in.at[1, k], right_recv.at[4 + k])
        part_in[lev, 1] = (right_in[1, 0] + right_in[1, 1]) + (right_in[1, 2] + right_in[1, 3])
        part(1, 1).start()

    @pl.when(jnp.logical_not(is_first))
    def _():
        from_before()

    totals = [kern[lev, n] for n in range(3)]
    for k in range(1, 4):
        d = lev ^ k
        arrived(mine_in.at[d], mine_recv.at[d])
        totals = [totals[n] + mine_in[d, n] for n in range(3)]
    t_all = t_mine
    for k in range(1, 4):
        arrived(t_lev.at[k], tl_recv.at[k])
        t_all = t_all + t_lev[k]
    obs_out[...] = t_all
    s_here = t_all * prec[...] * scale
    result = totals[2] * s_here + pltpu.roll(totals[0] * s_here, ny - 1, 1) + pltpu.roll(totals[1] * s_here, 1, 1)
    for k in range(4):
        arrived(left_in.at[k], left_recv.at[k])
    from_after = (left_in[0] + left_in[1]) + (left_in[2] + left_in[3])
    for k in range(4):
        arrived(t_right.at[k], tx_recv.at[4 + k])
    s_after = (t_right[0] + t_right[1]) + (t_right[2] + t_right[3])
    mine = rows_of(lev)
    out_buf[mine, :] = result + from_after * s_after
    gathers = [
        send(out_buf.at[mine], out_buf.at[mine], ag_send.at[k], ag_recv.at[lev], lev ^ k, tile) for k in range(1, 4)
    ]
    for copy in gathers:
        copy.start()

    @pl.when(is_first)
    def _():
        from_before()

    for d in range(4):
        @pl.when(d == lev_before)
        def _():
            halo(d).wait_send()
    for k in range(1, 4):
        spread(k).wait_send()
    for h in range(2):
        right(2 * h).wait_send()
        for to in (0, 2):
            right_both(2 * h + 1, to).wait_send()
    for copy in edges + t_sends:
        copy.wait_send()
    for c in range(4):
        @pl.when(c != lev)
        def _():
            mine_to(c).wait_send()
        left(c).wait_send()

    for copy in gathers:
        copy.wait_send()

    for k in range(1, 4):
        d = lev ^ k
        arrived(out_buf.at[rows_of(d)], ag_recv.at[d])
    arrived(part_in.at[lev ^ 1, 1], part_recv.at[4 + (lev ^ 1)])
    for k in range(1, 4):
        d = lev ^ k
        arrived(part_in.at[d, 0], part_recv.at[d])
    for k in range(1, 4):
        part(0, k).wait_send()
    part(1, 1).wait_send()
    for k in range(4):
        arrived(t_left.at[k], tx_recv.at[k])
    s_before = (t_left[0] + t_left[1]) + (t_left[2] + t_left[3])
    mask_row = mask[...].astype(F32)
    for h in range(2):
        rows = pl.ds((2 * h + 1) * chunk, chunk)
        hess_out[rows, 0, :] = mask_row * (out_buf[rows, :] + part_in[lev - core + h, 1] * s_before)
        rows = pl.ds(2 * h * chunk, chunk)
        hess_out[rows, 0, :] = mask_row * (out_buf[rows, :] + (part_in[h, 0] + part_in[2 + h, 0]) * s_before)


def per_device(
    control, emit_mask, bin_profile, plume_profile, courant, upwind, bin_speed, level_factor, background, coag_rate,
    obs_weight, obs_precision,
):
    nb, nl, _, ny = background.shape
    total = level_factor.shape[0]
    chunk = nb // 4
    vmem, dma = pltpu.VMEM, pltpu.SemaphoreType.DMA
    obs, hess = pl.pallas_call(
        functools.partial(kernel, nb, nl, total, 1.0 / (nb * total)),
        out_shape=(jax.ShapeDtypeStruct((1, ny), F32), jax.ShapeDtypeStruct((nb, 1, ny), F32)),
        in_specs=[pl.BlockSpec(memory_space=pl.ANY)] * 12,
        out_specs=(pl.BlockSpec(memory_space=pltpu.VMEM),) * 2,
        scratch_shapes=[
            vmem((nl, nb, ny), F32),
            vmem((nb, ny), F32),
            vmem((1, ny), jnp.int32),
            vmem((1, nb), F32),
            vmem((1, nl), F32),
            vmem((2, nl, ny), F32),
            vmem((2, nl, ny), jnp.int32),
            vmem((1, nb), F32),
            vmem((1, total), F32),
            vmem((nl, ny), F32),
            vmem((1, nb), F32),
            vmem((1, ny), F32),
            vmem((2 * nb, 256), BF16),
            vmem((nl, nb, ny), F32),
            vmem((nl + 1, nb, 128), F32),
            vmem((nl, nb, 128), F32),
            vmem((nl, nb, ny), F32),
            vmem((3, total, ny), F32),
            vmem((total, ny), F32),
            vmem((4, total, ny), F32),
            vmem((total, ny), F32),
            vmem((4, nl, ny), F32),
            vmem((nl, ny), F32),
            vmem((4, nb, ny), F32),
            vmem((nb, ny), F32),
            vmem((3, nb, ny), F32),
            vmem((2, nb, ny), F32),
            vmem((4, 4, chunk, ny), F32),
            vmem((nb, ny), F32),
            vmem((4, 3, chunk, ny), F32),
            vmem((4, chunk, ny), F32),
            vmem((2, 4, chunk, ny), F32),
            vmem((4, 2, chunk, ny), F32),
            vmem((4, 1, ny), F32),
            vmem((4, 1, ny), F32),
            vmem((4, 1, ny), F32),
            vmem((1, ny), F32),
            vmem((1, ny), F32),
            vmem((nb, ny), F32),
            dma((11,)), dma((nl,)),
            dma((4,)), dma((4,)), dma((4,)), dma((4,)), dma((2,)), dma((2,)),
            dma((4,)), dma((4,)), dma((4,)), dma((4,)), dma((8,)), dma((8,)),
            dma((8,)), dma((8,)), dma((4,)), dma((4,)), dma((8,)), dma((8,)), dma((4,)), dma((4,)),
            pltpu.SemaphoreType.REGULAR, pltpu.SemaphoreType.REGULAR, pltpu.SemaphoreType.REGULAR,
        ],
        compiler_params=pltpu.CompilerParams(collective_id=0, has_side_effects=True, vmem_limit_bytes=24 << 20),
        name="hessian",
    )(*[
        pltpu.with_memory_space_constraint(value, pltpu.HBM) for value in (
            control, emit_mask, bin_profile[None], plume_profile[None], courant, upwind, bin_speed[None],
            level_factor[None], background, coag_rate, obs_weight[None], obs_precision,
        )
    ])
    return obs, hess


def solution(mesh):
    in_specs = (
        P(None, "tile", None), P("tile", None), P(), P("lev"), P(None, "lev", "tile", None), P(None, "lev", "tile", None),
        P(), P(), P(None, "lev", "tile", None), P("lev", "tile", None), P(), P("tile", None),
    )
    out_specs = (P("tile", None), P(None, "tile", None))
    return jax.shard_map(per_device, mesh=mesh, in_specs=in_specs, out_specs=out_specs, check_vma=False)
```
